256 devices in a mesh: section: 4 (over y), dp: 64 (over x, z, core).
Axes of the slice: x: 4, y: 4, z: 8, core: 2. Of those that a mesh axis runs over, the one named last changes fastest.
Arguments:
- layer_out: bfloat16 [4, 16384, 5120], P('section', 'dp')
- input_grad: bfloat16 [4, 16384, 5120], P('section', 'dp')
- embedded: bfloat16 [16384, 5120], P('dp')
- loss_grad: bfloat16 [16384, 5120], P('dp')
- norm_gain: bfloat16 [4, 5120], P('section'), may hold values from 0.5 to 1.5
- prev_inverse: bfloat16 [4, 2, 40, 128, 128], P('section'), may hold values from -0.29882812 to 0.29882812
- plan: int32 [4, 32, 3], replicated, may hold values from 0 to 39, as said below
Outputs:
- inverse: bfloat16 [4, 2, 40, 128, 128], P('section')
The draws below stay inside these ranges and needn't reach their ends.
Inputs may be any that keep to these rules, and one draw needn't show every extreme that they name: plan[t, j] = (source section, factor 0 for activations or 1 for gradients, block) of the j-th block that section t inverts; no (source, factor, block) appears twice; a source is named at most 16 times in one section's list, and some source is named exactly 16 times in every section's list.
All inputs are finite; a program needn't handle non-finite values.
Results may differ from the reference program's by a relative error of at most 0.0024.
Values may be sent and summed in bfloat16 or wider, within the bound.
A program may use at most 128 MiB of HBM per device.

```python
import math
import jax
import jax.numpy as jnp
from jax import lax

D = 5120
BLK = 128
NBLK = 40
TOKENS = 16384
SLOTS = 32
N_SECTION = 4


def textured(key, shape, spread):
    k_normal = jax.random.fold_in(key, 0)
    k_cols = jax.random.fold_in(key, 2)
    k_rows = jax.random.fold_in(key, 3)
    normal_part = jax.random.normal(k_normal, shape, jnp.float32)
    base = normal_part
    mixed = base + 0.6 * jnp.roll(base, 1, axis=-1)
    col_scale = jnp.exp(jax.random.uniform(k_cols, (shape[0], 1, shape[2]), jnp.float32, math.log(0.4), math.log(2.5)))
    position = (jnp.arange(shape[1], dtype=jnp.float32) / (shape[1] - 1)).reshape(1, shape[1], 1)
    jitter = jax.random.uniform(k_rows, (shape[0], shape[1], 1), jnp.float32, -0.3, 0.3)
    row_scale = jnp.exp(spread * (2.0 * position - 1.0) + jitter)
    return (mixed * col_scale * row_scale).astype(jnp.bfloat16)


def draw_layer_out(key, part):
    key = jax.random.fold_in(key, 1)
    return textured(key, (N_SECTION, TOKENS, D), 0.7)


def draw_input_grad(key, part):
    key = jax.random.fold_in(key, 2)
    return textured(key, (N_SECTION, TOKENS, D), 0.7)


def draw_embedded(key, part):
    key = jax.random.fold_in(key, 3)
    return textured(key, (1, TOKENS, D), 0.7)[0]


def draw_loss_grad(key, part):
    key = jax.random.fold_in(key, 4)
    return textured(key, (1, TOKENS, D), 0.7)[0]


def draw_plan(key, part):
    key = jax.random.fold_in(key, 7)
    k_heavy, k_other, k_order, k_blocks = jax.random.split(key, 4)
    half = SLOTS // 2
    heavy = jax.random.randint(k_heavy, (), 0, N_SECTION)
    others = (heavy + 1 + jax.random.randint(k_other, (N_SECTION, SLOTS - half), 0, N_SECTION - 1)) % N_SECTION
    sources = jnp.concatenate([jnp.full((N_SECTION, half), heavy, jnp.int32), others.astype(jnp.int32)], 1)
    orders = jax.vmap(lambda k: jax.random.permutation(k, SLOTS))(jax.random.split(k_order, N_SECTION))
    sources = jnp.take_along_axis(sources, orders, 1)
    flat = sources.reshape(-1)
    onehot = (flat[:, None] == jnp.arange(N_SECTION, dtype=jnp.int32)[None, :]).astype(jnp.int32)
    ranks = jnp.sum((jnp.cumsum(onehot, 0) - onehot) * onehot, 1)
    tables = jax.vmap(lambda k: jax.random.permutation(k, 2 * NBLK))(jax.random.split(k_blocks, N_SECTION))
    picked = tables[flat, ranks].astype(jnp.int32)
    result = jnp.stack([flat, picked // NBLK, picked % NBLK], 1).reshape(N_SECTION, SLOTS, 3)
    return result.astype(jnp.int32)


def block_scale(stream_key, dims, cuts, low, high):
    level = 1.0
    for dim, parts in cuts:
        draws = jax.random.uniform(jax.random.fold_in(jax.random.fold_in(stream_key, 6), dim), (parts,), jnp.float32, low / len(cuts), high / len(cuts))
        level = level * jnp.repeat(jnp.exp(draws), dims[dim] // parts).reshape((-1,) + (1,) * (len(dims) - 1 - dim))
    return level


def scatter_about(stream_key, extent, width, most, cuts=(), kind=jnp.bfloat16):
    loudness = block_scale(stream_key, extent, cuts, -0.22, 0.18) if cuts else 1.0
    drawn = jax.random.normal(stream_key, extent, jnp.float32) * width * loudness
    return jnp.minimum(jnp.maximum(drawn, -most), most).astype(kind)


def setup_inputs(seed: int = 0) -> dict:
    key_of = jax.random.split(jax.random.key(seed), 8)
    layer_out = draw_layer_out(jax.random.fold_in(key_of[7], 71), 0)
    input_grad = draw_input_grad(jax.random.fold_in(key_of[7], 71), 0)
    embedded = draw_embedded(jax.random.fold_in(key_of[7], 71), 0)
    loss_grad = draw_loss_grad(jax.random.fold_in(key_of[7], 71), 0)
    norm_gain = jnp.clip(1.0 + 0.1 * jax.random.normal(key_of[4], (N_SECTION, D), jnp.float32), 0.5, 1.5).astype(jnp.bfloat16)
    prev_inverse = scatter_about(key_of[5], (N_SECTION, 2, NBLK, BLK, BLK), 0.05, 0.29882812, ((0, 4),))
    plan = draw_plan(jax.random.fold_in(key_of[7], 71), 0)
    return {"layer_out": layer_out, "input_grad": input_grad, "embedded": embedded, "loss_grad": loss_grad, "norm_gain": norm_gain, "prev_inverse": prev_inverse, "plan": plan}


damping = 0.1

def damped_inverse(blocks):
    size = blocks.shape[-1]
    eye = jnp.eye(size, dtype=blocks.dtype)
    lower = jnp.linalg.cholesky(blocks + damping * eye)
    left = jax.scipy.linalg.solve_triangular(lower, jnp.broadcast_to(eye, blocks.shape), lower=True)
    return jnp.einsum('...ji,...jk->...ik', left, left, precision=lax.Precision.HIGHEST)

def normed(inputs, gain):
    wide = inputs.astype(jnp.float32)
    scale = lax.rsqrt(lax.optimization_barrier(jnp.mean(wide * wide, axis=-1, keepdims=True)) + 1e-05)
    return (wide * scale * gain.astype(jnp.float32)[None, :]).astype(jnp.bfloat16)

def reference(layer_out, input_grad, embedded, loss_grad, norm_gain, prev_inverse, plan):
    act_list = []
    grad_list = []
    for section in range(N_SECTION):
        source = embedded if section == 0 else layer_out[section - 1]
        act_list.append(normed(source, norm_gain[section]))
        grad_list.append(loss_grad if section == N_SECTION - 1 else input_grad[section + 1])
    acts = jnp.stack(act_list)
    grads = jnp.stack(grad_list)
    entries = plan.reshape(N_SECTION * SLOTS, 3).astype(jnp.int32)

    def one(entry):
        anchor = entry[0].astype(jnp.int32)
        factor = entry[1]
        start = (entry[2] * BLK).astype(jnp.int32)
        zero = jnp.int32(0)
        col_a = lax.dynamic_slice(acts, (anchor, zero, start), (1, TOKENS, BLK))[0]
        col_g = lax.dynamic_slice(grads, (anchor, zero, start), (1, TOKENS, BLK))[0]
        column = jnp.where(factor == 0, col_a, col_g)
        fisher = jnp.dot(column.T.astype(jnp.float32), column.astype(jnp.float32), preferred_element_type=jnp.float32) / TOKENS
        return damped_inverse(fisher).astype(jnp.bfloat16)
    fresh = lax.map(one, entries)
    flat = prev_inverse.reshape(N_SECTION * 2 * NBLK, BLK, BLK)
    target = (entries[:, 0] * (2 * NBLK) + entries[:, 1] * NBLK + entries[:, 2]).astype(jnp.int32)
    flat = flat.at[target].set(fresh)
    return flat.reshape(prev_inverse.shape)
```

```python
import functools

import jax
import jax.numpy as jnp
from jax import lax
from jax.experimental import pallas as pl
from jax.experimental.pallas import tpu as pltpu
from jax.sharding import PartitionSpec as P

BLK = 128
NBLK = 40
ENTRIES = 128
NX, NZ, NC = 4, 8, 2
LEV = 5
PK = 72
ROWS = 256
TOKENS = 16384
damping = 0.1
MESH = pl.DeviceIdType.MESH
F32 = jnp.float32
BF16 = jnp.bfloat16
HI = lax.Precision.HIGHEST


def iota(shape, dim):
    return lax.broadcasted_iota(jnp.int32, shape, dim)


def pack(g):
    top, bottom = g[:64], g[64:]
    row, lane = iota((64, BLK), 0), iota((64, BLK), 1)
    turned = pltpu.roll(bottom, 64, 1)
    body = jnp.where((lane < 64) & (row > lane), turned, top)
    diag = jnp.where(lane - 64 == row, bottom, 0.0)
    corner = diag[0:8]
    for v in range(1, 8):
        corner = corner + diag[8 * v:8 * v + 8]
    return body, corner


def gram_kernel(plan, layer_out, input_grad, embedded, loss_grad, gain, prev,
                part, table, kept, xa, xg, scale, list_a, list_g, sems, ksem):
    sec = lax.axis_index("section")
    quarter = ROWS // 4

    def fetch(i, src, dst, at):
        rows = pl.ds(i * quarter, quarter)
        return pltpu.make_async_copy(src.at[rows], dst.at[rows], sems.at[at])

    @pl.when(sec == 3)
    def _():
        for i in range(4):
            fetch(i, embedded, xa, i).start()

    @pl.when(sec != 3)
    def _():
        for i in range(4):
            fetch(i, layer_out, xa, i).start()

    @pl.when(sec == 0)
    def _():
        for i in range(4):
            fetch(i, loss_grad, xg, 4 + i).start()

    @pl.when(sec != 0)
    def _():
        for i in range(4):
            fetch(i, input_grad, xg, 4 + i).start()

    keep = pltpu.make_async_copy(prev, kept, ksem)
    keep.start()

    src_a, src_g = lax.rem(sec + 1, 4), lax.rem(sec + 3, 4)

    def clear(i, _):
        table[i] = -1
        return 0

    lax.fori_loop(0, 2 * NBLK, clear, 0)

    def sort(e, c):
        na, ng, ma, mg = c
        s, f, k = plan[3 * e], plan[3 * e + 1], plan[3 * e + 2]
        hit_a = jnp.logical_and(s == src_a, f == 0)
        hit_g = jnp.logical_and(s == src_g, f == 1)
        mine = s == sec

        @pl.when(hit_a)
        def _():
            list_a[na] = k

        @pl.when(hit_g)
        def _():
            list_g[ng] = k

        @pl.when(mine)
        def _():
            r = jnp.where(f == 0, ma, 63 - mg)
            z, cc, x = lax.div(r, 8), lax.rem(lax.div(r, 4), 2), lax.rem(r, 4)
            table[f * NBLK + k] = cc * 32 + x * 8 + z

        one = jnp.int32(1)
        zero = jnp.int32(0)
        return (na + jnp.where(hit_a, one, zero), ng + jnp.where(hit_g, one, zero),
                ma + jnp.where(jnp.logical_and(mine, f == 0), one, zero),
                mg + jnp.where(jnp.logical_and(mine, f != 0), one, zero))

    z0 = jnp.int32(0)
    na, ng, ma, mg = lax.fori_loop(0, ENTRIES, sort, (z0, z0, z0, z0))
    table[80] = ma
    table[81] = mg

    for i in range(4):
        fetch(i, layer_out, xa, i).wait()

        @pl.loop(0, quarter // 16)
        def _(q):
            rows = pl.ds(pl.multiple_of(i * quarter + q * 16, 16), 16)
            acc = jnp.zeros((16, BLK), F32)
            for b in range(NBLK):
                v = xa[rows, b * BLK:(b + 1) * BLK].astype(F32)
                acc = acc + v * v
            mean = jnp.sum(acc, axis=1, keepdims=True) / (NBLK * BLK)
            scale[rows, :] = jnp.broadcast_to(lax.rsqrt(mean + 1e-05), (16, BLK))

    dims = (((0,), (0,)), ((), ()))

    def put(at, c):
        g = lax.dot_general(c, c, dims, preferred_element_type=F32)
        body, corner = pack(g)
        part[at, 0:64] = body
        part[at, 64:72] = corner

    @pl.loop(0, na)
    def _(n):
        k = list_a[n]
        cols = pl.ds(pl.multiple_of(k * BLK, BLK), BLK)
        c = (xa[:, cols].astype(F32) * scale[...] * gain[:, cols].astype(F32)).astype(BF16)
        z, cc, x = lax.div(n, 8), lax.rem(lax.div(n, 4), 2), lax.rem(n, 4)
        put(cc * 40 + x * 10 + z, c)

    for i in range(4):
        fetch(i, input_grad, xg, 4 + i).wait()

    @pl.loop(0, ng)
    def _(n):
        k = list_g[n]
        cols = pl.ds(pl.multiple_of(k * BLK, BLK), BLK)
        r = 63 - n
        z, cc, x = lax.div(r, 8), lax.rem(lax.div(r, 4), 2), lax.rem(r, 4)
        put(cc * 40 + x * 10 + 2 + z, xg[:, cols])

    keep.wait()


def gram(plan, layer_out, input_grad, embedded, loss_grad, gain, prev):
    any_ = pl.BlockSpec(memory_space=pl.ANY)
    smem = pl.BlockSpec(memory_space=pltpu.SMEM)
    vmem = pl.BlockSpec(memory_space=pltpu.VMEM)
    width = NBLK * BLK
    return pl.pallas_call(
        gram_kernel,
        out_shape=(pltpu.VMEM((80, PK, BLK), F32),
                   pltpu.SMEM((96,), jnp.int32),
                   pltpu.VMEM((2 * NBLK, BLK, BLK), BF16)),
        in_specs=[smem, any_, any_, any_, any_, vmem, any_],
        out_specs=(vmem, smem, vmem),
        scratch_shapes=[
            pltpu.VMEM((ROWS, width), BF16),
            pltpu.VMEM((ROWS, width), BF16),
            pltpu.VMEM((ROWS, BLK), F32),
            pltpu.SMEM((NBLK,), jnp.int32),
            pltpu.SMEM((NBLK,), jnp.int32),
            pltpu.SemaphoreType.DMA((8,)),
            pltpu.SemaphoreType.DMA,
        ],
        compiler_params=pltpu.CompilerParams(vmem_limit_bytes=40 * 2**20),
        name="gram",
    )(plan, *(pltpu.with_memory_space_constraint(a, pltpu.HBM) for a in (layer_out, input_grad, embedded, loss_grad)),
      gain, pltpu.with_memory_space_constraint(prev, pltpu.HBM))


def place():
    dp = lax.axis_index("dp")
    return lax.axis_index("section"), lax.div(dp, 16), lax.rem(lax.div(dp, 2), 8), lax.rem(dp, 2)


def dev(s, x, z, c):
    return (s, (x * NZ + z) * NC + c)


def greet(targets):
    barrier = pltpu.get_barrier_semaphore()
    for t in targets:
        pl.semaphore_signal(barrier, inc=1, device_id=t, device_id_type=MESH)
    pl.semaphore_wait(barrier, len(targets))


def remote(src, dst, ssem, rsem, to):
    return pltpu.make_async_remote_copy(src_ref=src, dst_ref=dst, send_sem=ssem, recv_sem=rsem,
                                        device_id=to, device_id_type=MESH)


def reduce_kernel(part, out_a, out_g, rc, rx, rza, rzg, s2, s3, ry,
                  cs, cr, xs, xr, zas, zar, zgs, zgr, ys, yr):
    s, x, z, c = place()
    mates = [dev(s, x, z, 1 - c)]
    xs_to = [dev(s, lax.rem(x + d, NX), z, c) for d in range(1, NX)]
    zs_to = [dev(s, x, lax.rem(z + d, NZ), c) for d in range(1, NZ)]
    ys_to = [dev(lax.rem(s + 1, 4), x, z, c), dev(lax.rem(s + 3, 4), x, z, c)]
    greet(mates + xs_to + zs_to + ys_to)
    order = [1, 3, 2, 0]
    core = []
    for n, d in enumerate(order):
        xt = lax.rem(x + d, NX)
        copy = remote(part.at[1 - c, xt], rc.at[n], cs.at[n], cr.at[n], mates[0])
        copy.start()
        core.append(copy)
    cross = []
    for n, d in enumerate(order):
        xt = lax.rem(x + d, NX)
        core[n].wait_recv()

        @pl.loop(0, 10)
        def _(i):
            rc[n, i] = rc[n, i] + part[c, xt, i]

        if d:
            copy = remote(rc.at[n], rx.at[d - 1], xs.at[d - 1], xr.at[d - 1], xs_to[d - 1])
            copy.start()
            cross.append(copy)
    for copy in cross:
        copy.wait_recv()

    @pl.loop(0, 10)
    def _(i):
        s2[i] = (rc[3, i] + rx[0, i]) + (rx[1, i] + rx[2, i])

    def to_a(d):
        zt = lax.rem(z + d, NZ)
        return zt, remote(s2.at[lax.min(zt, LEV - 1)], rza.at[d - 1], zas.at[d - 1], zar.at[d - 1], zs_to[d - 1])

    def to_g(d):
        zt = lax.rem(z + d, NZ)
        return zt, remote(s2.at[LEV + lax.max(zt - 3, 0)], rzg.at[d - 1], zgs.at[d - 1], zgr.at[d - 1], zs_to[d - 1])

    for d in (4, 3, 5, 2, 6, 1, 7):
        zt, copy = to_a(d)

        @pl.when(zt < LEV)
        def _():
            copy.start()

        zt, copy = to_g(d)

        @pl.when(zt >= NZ - LEV)
        def _():
            copy.start()

    ya = remote(s3.at[0], ry.at[0], ys.at[0], yr.at[0], ys_to[0])
    yg = remote(s3.at[1], ry.at[1], ys.at[1], yr.at[1], ys_to[1])

    @pl.when(z < LEV)
    def _():
        acc = s2[lax.min(z, LEV - 1)]
        for d in range(1, NZ):
            to_a(d)[1].wait_recv()
            acc = acc + rza[d - 1]
        s3[0] = acc
        ya.start()

    @pl.when(z >= NZ - LEV)
    def _():
        acc = s2[LEV + lax.max(z - 3, 0)]
        for d in range(1, NZ):
            to_g(d)[1].wait_recv()
            acc = acc + rzg[d - 1]
        s3[1] = acc
        yg.start()

    for copy in core:
        copy.wait_send()
    for copy in cross:
        copy.wait_send()
    for d in range(1, NZ):
        zt, copy = to_a(d)

        @pl.when(zt < LEV)
        def _():
            copy.wait_send()

        zt, copy = to_g(d)

        @pl.when(zt >= NZ - LEV)
        def _():
            copy.wait_send()

    @pl.when(z < LEV)
    def _():
        ya.wait()
        out_a[...] = ry[0]

    @pl.when(z >= LEV)
    def _():
        out_a[...] = jnp.zeros_like(out_a)

    @pl.when(z >= NZ - LEV)
    def _():
        yg.wait()
        out_g[...] = ry[1]

    @pl.when(z < NZ - LEV)
    def _():
        out_g[...] = jnp.zeros_like(out_g)


def reduce(part):
    vmem = pl.BlockSpec(memory_space=pltpu.VMEM)
    blk = pltpu.VMEM((PK, BLK), F32)
    dma = pltpu.SemaphoreType.DMA
    return pl.pallas_call(
        reduce_kernel,
        out_shape=(blk, blk),
        in_specs=[vmem],
        out_specs=(vmem, vmem),
        scratch_shapes=[
            pltpu.VMEM((4, 10, PK, BLK), F32),
            pltpu.VMEM((3, 10, PK, BLK), F32),
            pltpu.VMEM((7, PK, BLK), F32),
            pltpu.VMEM((7, PK, BLK), F32),
            pltpu.VMEM((10, PK, BLK), F32),
            pltpu.VMEM((2, PK, BLK), F32),
            pltpu.VMEM((2, PK, BLK), F32),
            dma((4,)), dma((4,)), dma((3,)), dma((3,)),
            dma((7,)), dma((7,)), dma((7,)), dma((7,)), dma((2,)), dma((2,)),
        ],
        compiler_params=pltpu.CompilerParams(collective_id=0, has_side_effects=True,
                                             vmem_limit_bytes=40 * 2**20),
        name="reduce",
    )(part.reshape(2, NX, 10, PK, BLK))


def unpack(p):
    row, lane = iota((64, BLK), 0), iota((64, BLK), 1)
    body, corner = p[:64], p[64:]
    top = jnp.where(row < lane, body, 0.0)
    low = jnp.where((row > lane), body, 0.0)
    bottom = pltpu.roll(low, 64, 1)
    off = jnp.concatenate([top, bottom], axis=0)
    diag_top = jnp.where(row == lane, body, 0.0)
    diag_bottom = jnp.where(lane - 64 == row, jnp.concatenate([corner] * 8, axis=0), 0.0)
    return off + off.T + jnp.concatenate([diag_top, diag_bottom], axis=0)


def mm(a, b):
    return jnp.dot(a.astype(BF16), b.astype(BF16), preferred_element_type=F32)


def mm32(a, b):
    return jnp.dot(a, b, preferred_element_type=F32, precision=HI)


def inverse_kernel(table, pa, pg, out, m_ref, x_ref):
    s, x, z, c = place()
    r = z * 8 + c * 4 + x
    na, ng = table[80], table[81]
    is_a = r < na
    used = jnp.logical_or(is_a, r >= 64 - ng)
    row, lane = iota((BLK, BLK), 0), iota((BLK, BLK), 1)
    eye = jnp.where(row == lane, 1.0, 0.0).astype(F32)

    @pl.when(jnp.logical_not(used))
    def _():
        out[...] = jnp.zeros_like(out)

    @pl.when(used)
    def _():
        m = unpack(jnp.where(is_a, pa[...], pg[...])) * (1.0 / TOKENS) + damping * eye
        d = jnp.where(row == lane, lax.rsqrt(m), 0.0)
        d_row = jnp.sum(d, axis=0, keepdims=True)
        d_col = jnp.sum(d, axis=1, keepdims=True)
        m = m * d_row * d_col
        m_ref[...] = m
        top = jnp.max(jnp.sum(jnp.abs(m), axis=0, keepdims=True), axis=1, keepdims=True)
        alpha = 1.8 / top
        p = eye - alpha * m
        y = eye + p
        for _ in range(6):
            p = mm(p, p)
            y = y + mm(y, p)
        y = alpha * y
        y = 0.5 * (y + y.T)
        e = eye - mm32(m, y)
        y = y + mm(y, e)
        e = eye - mm32(m, y)
        worst = jnp.max(jnp.abs(e))
        y = y + mm(y, e)
        y = 0.5 * (y + y.T)
        out[...] = (y * d_row * d_col).astype(BF16)

        @pl.when(jnp.logical_not(worst < 1e-3))
        def _():
            x_ref[...] = m_ref[...]

            def sweep(k, _):
                a = x_ref[...]
                r_k = x_ref[pl.ds(k, 1), :]
                c_k = jnp.sum(jnp.where(lane == k, a, 0.0), axis=1, keepdims=True)
                piv = jnp.sum(jnp.where(iota((1, BLK), 1) == k, r_k, 0.0), axis=1, keepdims=True)
                inv = 1.0 / piv
                new = a - c_k * (r_k * inv)
                new = jnp.where(row == k, r_k * inv, new)
                new = jnp.where(lane == k, c_k * inv, new)
                new = jnp.where(jnp.logical_and(row == k, lane == k), -inv, new)
                x_ref[...] = new
                return 0

            lax.fori_loop(0, BLK, sweep, 0)
            y = x_ref[...]
            y = -0.5 * (y + y.T)
            out[...] = (y * d_row * d_col).astype(BF16)


def inverse(table, pa, pg):
    vmem = pl.BlockSpec(memory_space=pltpu.VMEM)
    return pl.pallas_call(
        inverse_kernel,
        out_shape=pltpu.VMEM((BLK, BLK), BF16),
        in_specs=[pl.BlockSpec(memory_space=pltpu.SMEM), vmem, vmem],
        out_specs=vmem,
        scratch_shapes=[pltpu.VMEM((BLK, BLK), F32), pltpu.VMEM((BLK, BLK), F32)],
        compiler_params=pltpu.CompilerParams(vmem_limit_bytes=8 * 2**20),
        name="inverse",
    )(table, pa, pg)


def gather_kernel(mine, out, buf, zs, zr, xs, xr, cs, cr):
    s, x, z, c = place()
    mate = dev(s, x, z, 1 - c)
    xs_to = [dev(s, lax.rem(x + d, NX), z, c) for d in range(1, NX)]
    zs_to = [dev(s, x, lax.rem(z + d, NZ), c) for d in range(1, NZ)]
    greet([mate] + xs_to + zs_to)
    buf[c, x, z] = mine[...]
    around = []
    for d in (4, 3, 5, 2, 6, 1, 7):
        copy = remote(buf.at[c, x, z], buf.at[c, x, z], zs.at[d - 1], zr.at[d - 1], zs_to[d - 1])
        copy.start()
        around.append((d, copy))
    for d in (4, 3, 5, 2, 6, 1, 7):
        zf = lax.rem(z - d + NZ, NZ)
        remote(buf.at[c, x, zf], buf.at[c, x, zf], zs.at[d - 1], zr.at[d - 1], zs_to[d - 1]).wait_recv()
    cross = []
    for d in (2, 1, 3):
        copy = remote(buf.at[c, x], buf.at[c, x], xs.at[d - 1], xr.at[d - 1], xs_to[d - 1])
        copy.start()
        cross.append(copy)
    pair = [remote(buf.at[c, x], buf.at[c, x], cs.at[0], cr.at[0], mate)]
    pair[0].start()
    for d in (1, 3, 2):
        xf = lax.rem(x - d + NX, NX)
        remote(buf.at[c, xf], buf.at[c, xf], xs.at[d - 1], xr.at[d - 1], xs_to[d - 1]).wait_recv()
        copy = remote(buf.at[c, xf], buf.at[c, xf], cs.at[d], cr.at[d], mate)
        copy.start()
        pair.append(copy)
    for n, d in enumerate((0, 1, 3, 2)):
        xf = lax.rem(x - d + NX, NX)
        remote(buf.at[1 - c, xf], buf.at[1 - c, xf], cs.at[d], cr.at[d], mate).wait_recv()
    out[...] = buf[...]
    for d, copy in around:
        copy.wait_send()
    for copy in cross + pair:
        copy.wait_send()


def gather(mine):
    dma = pltpu.SemaphoreType.DMA
    shape = (NC, NX, NZ, BLK, BLK)
    return pl.pallas_call(
        gather_kernel,
        out_shape=pltpu.VMEM(shape, BF16),
        in_specs=[pl.BlockSpec(memory_space=pltpu.VMEM)],
        out_specs=pl.BlockSpec(memory_space=pltpu.VMEM),
        scratch_shapes=[pltpu.VMEM(shape, BF16), dma((7,)), dma((7,)), dma((3,)), dma((3,)),
                        dma((4,)), dma((4,))],
        compiler_params=pltpu.CompilerParams(collective_id=1, has_side_effects=True,
                                             vmem_limit_bytes=20 * 2**20),
        name="gather",
    )(mine)


def scatter_kernel(table, fresh, kept, out, buf, sems):
    step = 16

    def write(n):
        rows = pl.ds(n * step, step)
        return pltpu.make_async_copy(buf.at[rows], out.at[rows], sems.at[n])

    for n in range(2 * NBLK // step):
        for i in range(n * step, (n + 1) * step):
            at = table[i]

            @pl.when(at >= 0)
            def _():
                buf[i] = fresh[at]

            @pl.when(at < 0)
            def _():
                buf[i] = kept[i]

        write(n).start()
    for n in range(2 * NBLK // step):
        write(n).wait()


def scatter(table, fresh, kept):
    vmem = pl.BlockSpec(memory_space=pltpu.VMEM)
    shape = (2 * NBLK, BLK, BLK)
    return pl.pallas_call(
        scatter_kernel,
        out_shape=pltpu.HBM(shape, BF16),
        in_specs=[pl.BlockSpec(memory_space=pltpu.SMEM), vmem, vmem],
        out_specs=pl.BlockSpec(memory_space=pl.ANY),
        scratch_shapes=[pltpu.VMEM(shape, BF16), pltpu.SemaphoreType.DMA((5,))],
        compiler_params=pltpu.CompilerParams(vmem_limit_bytes=8 * 2**20),
        name="scatter",
    )(table, fresh, kept)


def body(layer_out, input_grad, embedded, loss_grad, norm_gain, prev_inverse, plan):
    gain = lax.ppermute(norm_gain, "section", [(i, (i + 3) % 4) for i in range(4)])
    part, table, kept = gram(plan.reshape(-1), layer_out[0], input_grad[0], embedded, loss_grad, gain,
                             prev_inverse.reshape(2 * NBLK, BLK, BLK))
    pa, pg = reduce(part)
    mine = inverse(table, pa, pg)
    every = gather(mine).reshape(64, BLK, BLK)
    return scatter(table, every, kept).reshape(prev_inverse.shape)


def solution(mesh):
    in_specs = (
        P("section", "dp", None),
        P("section", "dp", None),
        P("dp", None),
        P("dp", None),
        P("section", None),
        P("section", None, None, None, None),
        P(),
    )
    out_specs = P("section", None, None, None, None)
    return jax.shard_map(body, mesh=mesh, in_specs=in_specs, out_specs=out_specs, check_vma=False)
```

```python
import functools

import jax
import jax.numpy as jnp
from jax import lax
from jax.experimental import pallas as pl
from jax.experimental.pallas import tpu as pltpu
from jax.sharding import PartitionSpec as P

BLK = 128
NBLK = 40
ENTRIES = 128
NX, NZ, NC = 4, 8, 2
LEV = 5
PK = 72
ROWS = 256
TOKENS = 16384
UNROLL = 4
damping = 0.1
MESH = pl.DeviceIdType.MESH
F32 = jnp.float32
BF16 = jnp.bfloat16
HI = lax.Precision.HIGHEST


def iota(shape, dim):
    return lax.broadcasted_iota(jnp.int32, shape, dim)


def pack(g):
    top, bottom = g[:64], g[64:]
    row, lane = iota((64, BLK), 0), iota((64, BLK), 1)
    turned = pltpu.roll(bottom, 64, 1)
    body = jnp.where((lane < 64) & (row > lane), turned, top)
    diag = jnp.where(lane - 64 == row, bottom, 0.0)
    corner = diag[0:8]
    for v in range(1, 8):
        corner = corner + diag[8 * v:8 * v + 8]
    return body, corner


def chunk_of(r, g):
    z, cc, x = lax.div(r, 8), lax.rem(lax.div(r, 4), 2), lax.rem(r, 4)
    if g:
        q = jnp.where(z == 3, 4, z + 2)
    else:
        q = jnp.where(z == 4, 5, z)
    return (cc * 10 + q) * 4 + x


def gram_kernel(plan_at, layer_out, input_grad, embedded, loss_grad, gain_at, prev,
                part, table, kept, gvec, xa, xg, scale, plan, gain, list_a, list_g, my_k, sems, ksem, psem, gsem):
    listed = pltpu.make_async_copy(plan_at, plan, psem)
    listed.start()
    sec, mx, mz, mc = place()
    my_slot = mz * 8 + mc * 4 + mx
    quarter = ROWS // 4

    def fetch(i, src, dst, at):
        rows = pl.ds(i * quarter, quarter)
        return pltpu.make_async_copy(src.at[rows], dst.at[rows], sems.at[at])

    @pl.when(sec == 3)
    def _():
        for i in range(4):
            fetch(i, embedded, xa, i).start()

    @pl.when(sec != 3)
    def _():
        for i in range(4):
            fetch(i, layer_out, xa, i).start()

    @pl.when(sec == 0)
    def _():
        for i in range(4):
            fetch(i, loss_grad, xg, 4 + i).start()

    @pl.when(sec != 0)
    def _():
        for i in range(4):
            fetch(i, input_grad, xg, 4 + i).start()

    keep = pltpu.make_async_copy(prev, kept, ksem)
    keep.start()
    gains = pltpu.make_async_copy(gain_at, gain, gsem)
    gains.start()

    src_a, src_g = lax.rem(sec + 1, 4), lax.rem(sec + 3, 4)

    def clear(i, _):
        table[i] = -1
        return 0

    lax.fori_loop(0, 2 * NBLK, clear, 0)
    listed.wait()

    def sort(e, c):
        na, ng, ma, mg = c
        t, n = lax.div(e, 32), lax.rem(e, 32)
        s, f, k = plan[0, t, n], plan[1, t, n], plan[2, t, n]
        hit_a = jnp.logical_and(s == src_a, f == 0)
        hit_g = jnp.logical_and(s == src_g, f == 1)
        mine = s == sec

        @pl.when(jnp.logical_and(mine, jnp.logical_and(f == 0, ma == my_slot)))
        def _():
            my_k[0] = k

        @pl.when(hit_a)
        def _():
            list_a[na] = k

        @pl.when(hit_g)
        def _():
            list_g[ng] = k

        @pl.when(mine)
        def _():
            r = jnp.where(f == 0, ma, 63 - mg)
            z, cc, x = lax.div(r, 8), lax.rem(lax.div(r, 4), 2), lax.rem(r, 4)
            table[f * NBLK + k] = cc * 32 + x * 8 + z

        one = jnp.int32(1)
        zero = jnp.int32(0)
        return (na + jnp.where(hit_a, one, zero), ng + jnp.where(hit_g, one, zero),
                ma + jnp.where(jnp.logical_and(mine, f == 0), one, zero),
                mg + jnp.where(jnp.logical_and(mine, f != 0), one, zero))

    my_k[0] = 0
    z0 = jnp.int32(0)
    na, ng, ma, mg = lax.fori_loop(0, ENTRIES, sort, (z0, z0, z0, z0))
    table[80] = ma
    table[81] = mg

    for n in range(UNROLL - 1):
        list_a[na + n] = 0
        list_g[ng + n] = 0

    for i in range(4):
        fetch(i, layer_out, xa, i).wait()

        @pl.loop(0, quarter // 16)
        def _(q):
            rows = pl.ds(pl.multiple_of(i * quarter + q * 16, 16), 16)
            acc = jnp.zeros((16, BLK), F32)
            for b in range(NBLK):
                v = xa[rows, b * BLK:(b + 1) * BLK].astype(F32)
                acc = acc + v * v
            mean = jnp.sum(acc, axis=1, keepdims=True) / (NBLK * BLK)
            scale[rows, :] = jnp.broadcast_to(lax.rsqrt(mean + 1e-05), (16, BLK))

    dims = (((0,), (0,)), ((), ()))

    def several(count, names, column, at):
        @pl.loop(0, lax.div(count + (UNROLL - 1), UNROLL))
        def _(m):
            grams = []
            for u in range(UNROLL):
                k = names[m * UNROLL + u]
                c = column(pl.ds(pl.multiple_of(k * BLK, BLK), BLK))
                grams.append(lax.dot_general(c, c, dims, preferred_element_type=F32))
            for u in range(UNROLL):
                n = m * UNROLL + u
                body, corner = pack(grams[u])
                where = jnp.where(n < count, at(n), 80 + u)
                part[where, 0:64] = body
                part[where, 64:72] = corner

    several(na, list_a, lambda cols: (xa[:, cols].astype(F32) * scale[...]).astype(BF16), lambda n: chunk_of(n, 0))
    for i in range(4):
        fetch(i, input_grad, xg, 4 + i).wait()
    several(ng, list_g, lambda cols: xg[:, cols], lambda n: chunk_of(lax.max(63 - n, 24), 1))
    gains.wait()
    own = gain[:, pl.ds(pl.multiple_of(my_k[0] * BLK, BLK), BLK)].astype(F32)
    gvec[...] = jnp.broadcast_to(jnp.where(my_slot < ma, own, 1.0), (8, BLK))
    keep.wait()


def gram(plan, layer_out, input_grad, embedded, loss_grad, gain, prev):
    any_ = pl.BlockSpec(memory_space=pl.ANY)
    smem = pl.BlockSpec(memory_space=pltpu.SMEM)
    vmem = pl.BlockSpec(memory_space=pltpu.VMEM)
    width = NBLK * BLK
    return pl.pallas_call(
        gram_kernel,
        out_shape=(pltpu.VMEM((80 + UNROLL, PK, BLK), F32),
                   pltpu.SMEM((96,), jnp.int32),
                   pltpu.VMEM((2 * NBLK, BLK, BLK), BF16),
                   pltpu.VMEM((8, BLK), F32)),
        in_specs=[any_] * 7,
        out_specs=(vmem, smem, vmem, vmem),
        scratch_shapes=[
            pltpu.VMEM((ROWS, width), BF16),
            pltpu.VMEM((ROWS, width), BF16),
            pltpu.VMEM((ROWS, BLK), F32),
            pltpu.SMEM((3, 4, 32), jnp.int32),
            pltpu.VMEM((1, width), BF16),
            pltpu.SMEM((NBLK + UNROLL,), jnp.int32),
            pltpu.SMEM((NBLK + UNROLL,), jnp.int32),
            pltpu.SMEM((1,), jnp.int32),
            pltpu.SemaphoreType.DMA((8,)),
            pltpu.SemaphoreType.DMA,
            pltpu.SemaphoreType.DMA,
            pltpu.SemaphoreType.DMA,
        ],
        compiler_params=pltpu.CompilerParams(vmem_limit_bytes=40 * 2**20),
        name="gram",
    )(*(pltpu.with_memory_space_constraint(a, pltpu.HBM)
        for a in (plan, layer_out, input_grad, embedded, loss_grad, gain, prev)))


def place():
    dp = lax.axis_index("dp")
    return lax.axis_index("section"), lax.div(dp, 16), lax.rem(lax.div(dp, 2), 8), lax.rem(dp, 2)


def dev(s, x, z, c):
    return (s, (x * NZ + z) * NC + c)


def greet(targets):
    barrier = pltpu.get_barrier_semaphore()
    for t in targets:
        pl.semaphore_signal(barrier, inc=1, device_id=t, device_id_type=MESH)
    pl.semaphore_wait(barrier, len(targets))


def remote(src, dst, ssem, rsem, to):
    return pltpu.make_async_remote_copy(src_ref=src, dst_ref=dst, send_sem=ssem, recv_sem=rsem,
                                        device_id=to, device_id_type=MESH)


def z_of(q):
    g = jnp.logical_or(q == 4, q >= 6)
    return jnp.where(q <= 3, q, jnp.where(q <= 4, 3, jnp.where(q <= 6, 4, q - 2))), jnp.where(g, 1, 0)


def reduce_kernel(part, out_a, out_g, rc, d2, near, s2, rz, s3, ry,
                  cs, cr, ds, dr, ns, nr, zs, zr, ys, yr):
    s, x, z, c = place()
    mate = dev(s, x, z, 1 - c)
    right, left = lax.rem(x + 1, NX), lax.rem(x + 3, NX)
    across = lax.rem(x + 2, NX)
    sides = [dev(s, right, z, c), dev(s, left, z, c)]
    ys_to = [dev(lax.rem(s + 1, 4), x, z, c), dev(lax.rem(s + 3, 4), x, z, c)]
    greet([mate] + sides + [dev(s, x, lax.rem(z + d, NZ), c) for d in range(1, NZ)] + ys_to)
    zfirst = lax.rem(z + 2, NZ)
    q0 = jnp.where(zfirst <= 3, zfirst, jnp.where(zfirst == 4, 5, zfirst + 2))
    qs = [lax.rem(q0 + i, 10) for i in range(10)]

    def core(i):
        q = qs[i]
        return remote(part.at[pl.ds(((1 - c) * 10 + q) * 4, 4)], rc.at[i], cs.at[i], cr.at[i], mate)

    def far(i):
        return remote(rc.at[i, across], d2.at[i], ds.at[i], dr.at[i], sides[i % 2])

    def beside(i, w):
        return remote(rc.at[i, (right, left)[w]], near.at[w, i], ns.at[w, i], nr.at[w, i], sides[w])

    def up(i):
        q = qs[i]
        zt, g = z_of(q)
        d = lax.rem(zt - z + NZ, NZ)
        at = lax.max(d - 1, 0)
        to = dev(s, x, zt, c)
        return d, remote(s2.at[i], rz.at[g, at], zs.at[g, at], zr.at[g, at], to)

    for i in range(10):
        core(i).start()

    def first(i):
        core(i).wait_recv()
        base = (c * 10 + qs[i]) * 4
        rc[i, across] = rc[i, across] + part[base + across]
        far(i).start()
        other = (left, right)[i % 2]
        rc[i, other] = rc[i, other] + part[base + other]
        beside(i, 1 - i % 2).start()
        one = (right, left)[i % 2]
        rc[i, one] = rc[i, one] + part[base + one]
        rc[i, x] = rc[i, x] + part[base + x]

    def second(i):
        far(i).wait_recv()
        one = (right, left)[i % 2]
        rc[i, one] = rc[i, one] + d2[i]
        beside(i, i % 2).start()

    def third(i):
        beside(i, 0).wait_recv()
        beside(i, 1).wait_recv()
        s2[i] = rc[i, x] + (near[0, i] + near[1, i])
        d, copy = up(i)

        @pl.when(d > 0)
        def _():
            copy.start()

        zt, g = z_of(qs[i])

        @pl.when(d == 0)
        def _():
            s3[g] = s2[i]

    for i in range(14):
        if i < 10:
            first(i)
        if 2 <= i < 12:
            second(i - 2)
        if i >= 4:
            third(i - 4)

    ya = remote(s3.at[0], ry.at[0], ys.at[0], yr.at[0], ys_to[0])
    yg = remote(s3.at[1], ry.at[1], ys.at[1], yr.at[1], ys_to[1])
    has_a, has_g = z < LEV, z >= NZ - LEV

    def finish(g, copy):
        acc = s3[g]
        for d in (7, 6, 5, 4, 3, 2, 1):
            remote(s2.at[0], rz.at[g, d - 1], zs.at[g, d - 1], zr.at[g, d - 1], mate).wait_recv()
            acc = acc + rz[g, d - 1]
        s3[g] = acc
        copy.start()

    @pl.when(has_a)
    def _():
        finish(0, ya)

    @pl.when(has_g)
    def _():
        finish(1, yg)

    for i in range(10):
        core(i).wait_send()
        far(i).wait_send()
        beside(i, 0).wait_send()
        beside(i, 1).wait_send()
        d, copy = up(i)

        @pl.when(d > 0)
        def _():
            copy.wait_send()

    @pl.when(has_a)
    def _():
        ya.wait()
        out_a[...] = ry[0]

    @pl.when(jnp.logical_not(has_a))
    def _():
        out_a[...] = jnp.zeros_like(out_a)

    @pl.when(has_g)
    def _():
        yg.wait()
        out_g[...] = ry[1]

    @pl.when(jnp.logical_not(has_g))
    def _():
        out_g[...] = jnp.zeros_like(out_g)


def reduce(part):
    vmem = pl.BlockSpec(memory_space=pltpu.VMEM)
    blk = pltpu.VMEM((PK, BLK), F32)
    dma = pltpu.SemaphoreType.DMA
    return pl.pallas_call(
        reduce_kernel,
        out_shape=(blk, blk),
        in_specs=[vmem],
        out_specs=(vmem, vmem),
        scratch_shapes=[
            pltpu.VMEM((10, 4, PK, BLK), F32),
            pltpu.VMEM((10, PK, BLK), F32),
            pltpu.VMEM((2, 10, PK, BLK), F32),
            pltpu.VMEM((10, PK, BLK), F32),
            pltpu.VMEM((2, 7, PK, BLK), F32),
            pltpu.VMEM((2, PK, BLK), F32),
            pltpu.VMEM((2, PK, BLK), F32),
            dma((10,)), dma((10,)), dma((10,)), dma((10,)), dma((2, 10)), dma((2, 10)),
            dma((2, 7)), dma((2, 7)), dma((2,)), dma((2,)),
        ],
        compiler_params=pltpu.CompilerParams(collective_id=0, has_side_effects=True,
                                             vmem_limit_bytes=24 * 2**20),
        name="reduce",
    )(part)


def unpack(p):
    row, lane = iota((64, BLK), 0), iota((64, BLK), 1)
    body, corner = p[:64], p[64:]
    top = jnp.where(row < lane, body, 0.0)
    low = jnp.where((row > lane), body, 0.0)
    bottom = pltpu.roll(low, 64, 1)
    off = jnp.concatenate([top, bottom], axis=0)
    diag_top = jnp.where(row == lane, body, 0.0)
    diag_bottom = jnp.where(lane - 64 == row, jnp.concatenate([corner] * 8, axis=0), 0.0)
    return off + off.T + jnp.concatenate([diag_top, diag_bottom], axis=0)


def mm(a, b):
    return jnp.dot(a.astype(BF16), b.astype(BF16), preferred_element_type=F32)


def mm32(a, b):
    return jnp.dot(a, b, preferred_element_type=F32, precision=HI)


def inverse_kernel(table, pa, pg, gvec, out, m_ref, x_ref):
    s, x, z, c = place()
    r = z * 8 + c * 4 + x
    na, ng = table[80], table[81]
    is_a = r < na
    used = jnp.logical_or(is_a, r >= 64 - ng)
    row, lane = iota((BLK, BLK), 0), iota((BLK, BLK), 1)
    eye = jnp.where(row == lane, 1.0, 0.0).astype(F32)

    @pl.when(jnp.logical_not(used))
    def _():
        out[...] = jnp.zeros_like(out)

    @pl.when(used)
    def _():
        g_row = gvec[0:1]
        g_col = jnp.sum(g_row * eye, axis=1, keepdims=True)
        m = unpack(jnp.where(is_a, pa[...], pg[...])) * (1.0 / TOKENS)
        m = m * g_row * g_col + damping * eye
        d = jnp.where(row == lane, lax.rsqrt(m), 0.0)
        d_row = jnp.sum(d, axis=0, keepdims=True)
        d_col = jnp.sum(d, axis=1, keepdims=True)
        m = m * d_row * d_col
        m_ref[...] = m
        top = jnp.max(jnp.sum(jnp.abs(m), axis=0, keepdims=True), axis=1, keepdims=True)
        alpha = 1.8 / top
        p = eye - alpha * m
        y = eye + p
        for _ in range(6):
            p = mm(p, p)
            y = y + mm(y, p)
        y = alpha * y
        y = 0.5 * (y + y.T)
        e = eye - mm32(m, y)
        y = y + mm(y, e)
        e = eye - mm32(m, y)
        worst = jnp.max(jnp.abs(e))
        y = y + mm(y, e)
        y = 0.5 * (y + y.T)
        out[...] = (y * d_row * d_col).astype(BF16)

        @pl.when(jnp.logical_not(worst < 1e-3))
        def _():
            x_ref[...] = m_ref[...]

            def sweep(k, _):
                a = x_ref[...]
                r_k = x_ref[pl.ds(k, 1), :]
                c_k = jnp.sum(jnp.where(lane == k, a, 0.0), axis=1, keepdims=True)
                piv = jnp.sum(jnp.where(iota((1, BLK), 1) == k, r_k, 0.0), axis=1, keepdims=True)
                inv = 1.0 / piv
                new = a - c_k * (r_k * inv)
                new = jnp.where(row == k, r_k * inv, new)
                new = jnp.where(lane == k, c_k * inv, new)
                new = jnp.where(jnp.logical_and(row == k, lane == k), -inv, new)
                x_ref[...] = new
                return 0

            lax.fori_loop(0, BLK, sweep, 0)
            y = x_ref[...]
            y = -0.5 * (y + y.T)
            out[...] = (y * d_row * d_col).astype(BF16)


def inverse(table, pa, pg, gvec):
    vmem = pl.BlockSpec(memory_space=pltpu.VMEM)
    return pl.pallas_call(
        inverse_kernel,
        out_shape=pltpu.VMEM((BLK, BLK), BF16),
        in_specs=[pl.BlockSpec(memory_space=pltpu.SMEM), vmem, vmem, vmem],
        out_specs=vmem,
        scratch_shapes=[pltpu.VMEM((BLK, BLK), F32), pltpu.VMEM((BLK, BLK), F32)],
        compiler_params=pltpu.CompilerParams(vmem_limit_bytes=8 * 2**20),
        name="inverse",
    )(table, pa, pg, gvec)


def gather_kernel(mine, out, zs, zr, ns, nr, fs, fr, cs, cr):
    s, x, z, c = place()
    mate = dev(s, x, z, 1 - c)
    right, left, across = lax.rem(x + 1, NX), lax.rem(x + 3, NX), lax.rem(x + 2, NX)
    sides = [dev(s, right, z, c), dev(s, left, z, c)]
    greet([mate] + sides + [dev(s, x, lax.rem(z + d, NZ), c) for d in range(1, NZ)])
    out[c, x, z] = mine[...]
    order = (0, 1, 7, 2, 6, 3, 5, 4)

    def along(d):
        to = dev(s, x, lax.rem(z + d, NZ), c)
        return remote(out.at[c, x, z], out.at[c, x, z], zs.at[d], zr.at[d], to)

    def block(xf, i):
        return out.at[c, xf, lax.rem(z - order[i] + NZ, NZ)]

    def beside(i, w):
        return remote(block(x, i), block(x, i), ns.at[w, i], nr.at[w, i], sides[w])

    def came(i, w):
        at = block((left, right)[w], i)
        return at, remote(at, at, ns.at[w, i], nr.at[w, i], sides[w])

    def on(i):
        w = i % 2
        at = block((left, right)[w], i)
        return remote(at, at, fs.at[i], fr.at[i], sides[w])

    def pair(xf, k, i):
        at = block(xf, i)
        return remote(at, at, cs.at[k, i], cr.at[k, i], mate)

    def mirror(xf, k, i):
        at = out.at[1 - c, xf, lax.rem(z - order[i] + NZ, NZ)]
        return remote(at, at, cs.at[k, i], cr.at[k, i], mate)

    for d in order[1:]:
        along(d).start()

    def first(i):
        d = order[i]
        if d:
            at = block(x, i)
            remote(at, at, zs.at[d], zr.at[d], mate).wait_recv()
        beside(i, 0).start()
        beside(i, 1).start()
        pair(x, 0, i).start()

    def second(i):
        w = i % 2
        came(i, w)[1].wait_recv()
        on(i).start()
        pair((left, right)[w], 1, i).start()
        came(i, 1 - w)[1].wait_recv()
        pair((right, left)[w], 2, i).start()

    def third(i):
        at = block(across, i)
        remote(at, at, fs.at[i], fr.at[i], mate).wait_recv()
        pair(across, 3, i).start()

    for i in range(12):
        if i < 8:
            first(i)
        if 2 <= i < 10:
            second(i - 2)
        if i >= 4:
            third(i - 4)

    for i in range(8):
        w = i % 2
        for k, xf in enumerate((x, (left, right)[w], (right, left)[w], across)):
            mirror(xf, k, i).wait_recv()
    for d in order[1:]:
        along(d).wait_send()
    for i in range(8):
        w = i % 2
        beside(i, 0).wait_send()
        beside(i, 1).wait_send()
        on(i).wait_send()
        for k, xf in enumerate((x, (left, right)[w], (right, left)[w], across)):
            pair(xf, k, i).wait_send()


def gather(mine):
    dma = pltpu.SemaphoreType.DMA
    shape = (NC, NX, NZ, BLK, BLK)
    vmem = pl.BlockSpec(memory_space=pltpu.VMEM)
    return pl.pallas_call(
        gather_kernel,
        out_shape=pltpu.VMEM(shape, BF16),
        in_specs=[vmem],
        out_specs=vmem,
        scratch_shapes=[dma((8,)), dma((8,)), dma((2, 8)), dma((2, 8)), dma((8,)), dma((8,)),
                        dma((4, 8)), dma((4, 8))],
        compiler_params=pltpu.CompilerParams(collective_id=1, has_side_effects=True,
                                             vmem_limit_bytes=8 * 2**20),
        name="gather",
    )(mine)


def scatter_kernel(table, fresh, kept, out, buf, sems):
    step = 16

    def write(n):
        rows = pl.ds(n * step, step)
        return pltpu.make_async_copy(buf.at[rows], out.at[rows], sems.at[n])

    for n in range(2 * NBLK // step):
        for i in range(n * step, (n + 1) * step):
            at = table[i]

            @pl.when(at >= 0)
            def _():
                buf[i] = fresh[at]

            @pl.when(at < 0)
            def _():
                buf[i] = kept[i]

        write(n).start()
    for n in range(2 * NBLK // step):
        write(n).wait()


def scatter(table, fresh, kept):
    vmem = pl.BlockSpec(memory_space=pltpu.VMEM)
    shape = (2 * NBLK, BLK, BLK)
    return pl.pallas_call(
        scatter_kernel,
        out_shape=pltpu.HBM(shape, BF16),
        in_specs=[pl.BlockSpec(memory_space=pltpu.SMEM), vmem, vmem],
        out_specs=pl.BlockSpec(memory_space=pl.ANY),
        scratch_shapes=[pltpu.VMEM(shape, BF16), pltpu.SemaphoreType.DMA((5,))],
        compiler_params=pltpu.CompilerParams(vmem_limit_bytes=8 * 2**20),
        name="scatter",
    )(table, fresh, kept)


def body(layer_out, input_grad, embedded, loss_grad, norm_gain, prev_inverse, plan):
    part, table, kept, gvec = gram(plan.transpose(2, 0, 1), layer_out[0], input_grad[0], embedded, loss_grad,
                                   norm_gain, prev_inverse.reshape(2 * NBLK, BLK, BLK))
    pa, pg = reduce(part)
    mine = inverse(table, pa, pg, gvec)
    every = gather(mine).reshape(64, BLK, BLK)
    return scatter(table, every, kept).reshape(prev_inverse.shape)


def solution(mesh):
    in_specs = (
        P("section", "dp", None),
        P("section", "dp", None),
        P("dp", None),
        P("dp", None),
        P("section", None),
        P("section", None, None, None, None),
        P(),
    )
    out_specs = P("section", None, None, None, None)
    return jax.shard_map(body, mesh=mesh, in_specs=in_specs, out_specs=out_specs, check_vma=False)
```

```python
import functools

import jax
import jax.numpy as jnp
from jax import lax
from jax.experimental import pallas as pl
from jax.experimental.pallas import tpu as pltpu
from jax.sharding import PartitionSpec as P

BLK = 128
NBLK = 40
ENTRIES = 128
NX, NZ, NC = 4, 8, 2
LEV = 5
PK = 72
ROWS = 256
TOKENS = 16384
damping = 0.1
MESH = pl.DeviceIdType.MESH
F32 = jnp.float32
BF16 = jnp.bfloat16
HI = lax.Precision.HIGHEST


def iota(shape, dim):
    return lax.broadcasted_iota(jnp.int32, shape, dim)


def pack(g):
    top, bottom = g[:64], g[64:]
    row, lane = iota((64, BLK), 0), iota((64, BLK), 1)
    turned = pltpu.roll(bottom, 64, 1)
    body = jnp.where((lane < 64) & (row > lane), turned, top)
    diag = jnp.where(lane - 64 == row, bottom, 0.0)
    corner = diag[0:8]
    for v in range(1, 8):
        corner = corner + diag[8 * v:8 * v + 8]
    return body, corner


def chunk_of(r, g):
    z = r >> 3
    q = jnp.where(z == 3, 4, z + 2) if g else jnp.where(z == 4, 5, z)
    return (((r >> 2) & 1) * 10 + q) * 4 + (r & 3)


def load_kernel(plan_at, layer_out, input_grad, embedded, loss_grad, gain_at,
                names, table, gvec, xs, xa, plan, gain, slot_k, sems, xsem, psem, gsem):
    listed = pltpu.make_async_copy(plan_at, plan, psem)
    listed.start()
    sec, mx, mz, mc = place()
    my_slot = mz * 8 + mc * 4 + mx
    quarter = ROWS // 4

    def fetch(i, src):
        rows = pl.ds(i * quarter, quarter)
        return pltpu.make_async_copy(src.at[rows], xa.at[rows], sems.at[i])

    def stripes(src):
        for b in range(NBLK):
            pltpu.make_async_copy(src.at[:, b * BLK:(b + 1) * BLK], xs.at[1, b], xsem).start()

    @pl.when(sec == 3)
    def _():
        for i in range(4):
            fetch(i, embedded).start()

    @pl.when(sec != 3)
    def _():
        for i in range(4):
            fetch(i, layer_out).start()

    @pl.when(sec == 0)
    def _():
        stripes(loss_grad)

    @pl.when(sec != 0)
    def _():
        stripes(input_grad)

    gains = pltpu.make_async_copy(gain_at, gain, gsem)
    gains.start()
    src_a, src_g = (sec + 1) & 3, (sec + 3) & 3

    def clear(i, _):
        for u in range(8):
            table[i * 8 + u] = -1
            names[i * 8 + u] = 0
        return 0

    lax.fori_loop(0, 10, clear, 0)
    listed.wait()
    one, zero = jnp.int32(1), jnp.int32(0)

    def sort(e, c):
        na, ng, ma, mg = c
        for u in range(8):
            t, n = e >> 2, (e & 3) * 8 + u
            s, f, k = plan[0, t, n], plan[1, t, n], plan[2, t, n]
            act = f == 0
            hit_a = jnp.logical_and(s == src_a, act)
            hit_g = jnp.logical_and(s == src_g, jnp.logical_not(act))
            mine_a = jnp.logical_and(s == sec, act)
            mine_g = jnp.logical_and(s == sec, jnp.logical_not(act))
            at = jnp.where(hit_a, chunk_of(na, 0), jnp.where(hit_g, chunk_of(63 - ng, 1), 80))
            names[at] = k
            slot_k[jnp.where(mine_a, ma, 64)] = k
            r = jnp.where(act, ma, 63 - mg)
            where = ((r >> 2) & 1) * 32 + (r & 3) * 8 + (r >> 3)
            table[jnp.where(s == sec, jnp.where(act, k, NBLK + k), 95)] = where
            na, ng = na + jnp.where(hit_a, one, zero), ng + jnp.where(hit_g, one, zero)
            ma, mg = ma + jnp.where(mine_a, one, zero), mg + jnp.where(mine_g, one, zero)
        return na, ng, ma, mg

    slot_k[my_slot] = 0
    na, ng, ma, mg = lax.fori_loop(0, ENTRIES // 8, sort, (zero, zero, zero, zero))
    table[80] = ma
    table[81] = mg

    for i in range(4):
        fetch(i, layer_out).wait()

        @pl.loop(0, quarter // 32)
        def _(q):
            rows = pl.ds(pl.multiple_of(i * quarter + q * 32, 32), 32)
            acc = [jnp.zeros((32, BLK), F32) for _ in range(2)]
            for b in range(NBLK):
                v = xa[rows, b * BLK:(b + 1) * BLK].astype(F32)
                acc[b % 2] = acc[b % 2] + v * v
            mean = jnp.sum(acc[0] + acc[1], axis=1, keepdims=True) / (NBLK * BLK)
            scale = jnp.broadcast_to(lax.rsqrt(mean + 1e-05), (32, BLK))
            for b in range(NBLK):
                v = xa[rows, b * BLK:(b + 1) * BLK].astype(F32)
                xs[0, b, rows, :] = (v * scale).astype(BF16)

    gains.wait()
    own = gain[:, pl.ds(pl.multiple_of(slot_k[my_slot] * BLK, BLK), BLK)].astype(F32)
    gvec[...] = jnp.broadcast_to(jnp.where(my_slot < ma, own, 1.0), (8, BLK))
    pltpu.make_async_copy(xs.at[0], xs.at[1], xsem).wait()


def load(plan, layer_out, input_grad, embedded, loss_grad, gain):
    any_ = pl.BlockSpec(memory_space=pl.ANY)
    smem = pl.BlockSpec(memory_space=pltpu.SMEM)
    vmem = pl.BlockSpec(memory_space=pltpu.VMEM)
    width = NBLK * BLK
    return pl.pallas_call(
        load_kernel,
        out_shape=(pltpu.SMEM((96,), jnp.int32),
                   pltpu.SMEM((96,), jnp.int32),
                   pltpu.VMEM((8, BLK), F32),
                   pltpu.VMEM((2, NBLK, ROWS, BLK), BF16)),
        in_specs=[any_] * 6,
        out_specs=(smem, smem, vmem, vmem),
        scratch_shapes=[
            pltpu.VMEM((ROWS, width), BF16),
            pltpu.SMEM((3, 4, 32), jnp.int32),
            pltpu.VMEM((1, width), BF16),
            pltpu.SMEM((72,), jnp.int32),
            pltpu.SemaphoreType.DMA((4,)),
            pltpu.SemaphoreType.DMA,
            pltpu.SemaphoreType.DMA,
            pltpu.SemaphoreType.DMA,
        ],
        compiler_params=pltpu.CompilerParams(vmem_limit_bytes=8 * 2**20),
        name="load",
    )(*(pltpu.with_memory_space_constraint(a, pltpu.HBM)
        for a in (plan, layer_out, input_grad, embedded, loss_grad, gain)))


def place():
    dp = lax.axis_index("dp")
    return lax.axis_index("section"), lax.div(dp, 16), lax.rem(lax.div(dp, 2), 8), lax.rem(dp, 2)


def dev(s, x, z, c):
    return (s, (x * NZ + z) * NC + c)


def greet(targets):
    barrier = pltpu.get_barrier_semaphore()
    for t in targets:
        pl.semaphore_signal(barrier, inc=1, device_id=t, device_id_type=MESH)
    pl.semaphore_wait(barrier, len(targets))


def remote(src, dst, ssem, rsem, to):
    return pltpu.make_async_remote_copy(src_ref=src, dst_ref=dst, send_sem=ssem, recv_sem=rsem,
                                        device_id=to, device_id_type=MESH)


def z_of(q):
    g = jnp.logical_or(q == 4, q >= 6)
    return jnp.where(q <= 3, q, jnp.where(q <= 4, 3, jnp.where(q <= 6, 4, q - 2))), jnp.where(g, 1, 0)


def reduce_kernel(names, xs, out_a, out_g, away, own, rc, d2, near, s2, rz,
                  cs, cr, ds, dr, ns, nr, zs, zr):
    s, x, z, c = place()
    mate = dev(s, x, z, 1 - c)
    right, left = lax.rem(x + 1, NX), lax.rem(x + 3, NX)
    across = lax.rem(x + 2, NX)
    ahead, behind = lax.rem(s + 1, 4), lax.rem(s + 3, 4)
    has_a, has_g = z < LEV, z >= NZ - LEV
    barrier = pltpu.get_barrier_semaphore()

    def hail(t):
        pl.semaphore_signal(barrier, inc=1, device_id=t, device_id_type=MESH)

    for t in (mate, dev(s, right, z, c), dev(s, left, z, c)):
        hail(t)

    @pl.when(has_a)
    def _():
        for zf in range(NZ):
            hail(dev(behind, x, zf, c))

    @pl.when(has_g)
    def _():
        for zf in range(NZ):
            hail(dev(ahead, x, zf, c))

    zfirst = lax.rem(z + 2, NZ)
    q0 = jnp.where(zfirst <= 3, zfirst, jnp.where(zfirst == 4, 5, zfirst + 2))

    def way(i):
        w = lax.rem(i, 2)
        return jnp.where(w == 0, right, left), jnp.where(w == 0, left, right), w

    def core(i):
        return remote(away.at[i], rc.at[i], cs.at[i], cr.at[i], mate)

    def far(i):
        return remote(rc.at[i, across], d2.at[i], ds.at[i], dr.at[i], dev(s, way(i)[0], z, c))

    def beside(i, xt, w):
        return remote(rc.at[i, xt], near.at[w, i], ns.at[w, i], nr.at[w, i], dev(s, xt, z, c))

    def up(i):
        zt, g = z_of(lax.rem(q0 + i, 10))
        to = dev(jnp.where(g == 0, ahead, behind), x, zt, c)
        return remote(s2.at[i], rz.at[g, z], zs.at[i], zr.at[g, z], to)

    dims = (((0,), (0,)), ((), ()))

    def grams(i, cc, into):
        q = lax.rem(q0 + i, 10)
        g = z_of(q)[1]
        found = []
        for xt in range(NX):
            k = names[(cc * 10 + q) * 4 + xt]
            col = xs[g, k]
            found.append(lax.dot_general(col, col, dims, preferred_element_type=F32))
        for xt in range(NX):
            body, corner = pack(found[xt])
            into[i, xt, 0:64] = body
            into[i, xt, 64:72] = corner

    def first(i):
        core(i).wait_recv()
        one, other, w = way(i)
        rc[i, across] = rc[i, across] + own[i, across]
        far(i).start()
        rc[i, other] = rc[i, other] + own[i, other]
        beside(i, other, 1 - w).start()
        rc[i, one] = rc[i, one] + own[i, one]
        rc[i, x] = rc[i, x] + own[i, x]

    def second(i):
        far(i).wait_recv()
        one, _, w = way(i)
        rc[i, one] = rc[i, one] + d2[i]
        beside(i, one, w).start()

    def third(i):
        beside(i, right, 0).wait_recv()
        beside(i, left, 1).wait_recv()
        s2[i] = rc[i, x] + (near[0, i] + near[1, i])
        up(i).start()

    grams(0, 1 - c, away)
    grams(1, 1 - c, away)
    pl.semaphore_wait(barrier, 13)
    core(0).start()
    core(1).start()

    def step(i, _):
        @pl.when(i < 8)
        def _():
            grams(i + 2, 1 - c, away)
            core(i + 2).start()

        @pl.when(i < 10)
        def _():
            grams(i, c, own)
            first(i)

        @pl.when(jnp.logical_and(i >= 2, i < 12))
        def _():
            second(i - 2)

        @pl.when(i >= 4)
        def _():
            third(i - 4)

        return 0

    lax.fori_loop(0, 14, step, 0)

    def total(g, out):
        for zf in range(NZ):
            remote(s2.at[0], rz.at[g, zf], zs.at[0], zr.at[g, zf], mate).wait_recv()
        out[...] = ((rz[g, 0] + rz[g, 1]) + (rz[g, 2] + rz[g, 3])) + ((rz[g, 4] + rz[g, 5]) + (rz[g, 6] + rz[g, 7]))

    @pl.when(has_a)
    def _():
        total(0, out_a)

    @pl.when(jnp.logical_not(has_a))
    def _():
        out_a[...] = jnp.zeros_like(out_a)

    @pl.when(has_g)
    def _():
        total(1, out_g)

    @pl.when(jnp.logical_not(has_g))
    def _():
        out_g[...] = jnp.zeros_like(out_g)

    def sent(i, _):
        core(i).wait_send()
        far(i).wait_send()
        beside(i, right, 0).wait_send()
        beside(i, left, 1).wait_send()
        up(i).wait_send()
        return 0

    lax.fori_loop(0, 10, sent, 0)


def reduce(names, xs):
    vmem = pl.BlockSpec(memory_space=pltpu.VMEM)
    blk = pltpu.VMEM((PK, BLK), F32)
    dma = pltpu.SemaphoreType.DMA
    return pl.pallas_call(
        reduce_kernel,
        out_shape=(blk, blk),
        in_specs=[pl.BlockSpec(memory_space=pltpu.SMEM), vmem],
        out_specs=(vmem, vmem),
        scratch_shapes=[
            pltpu.VMEM((10, 4, PK, BLK), F32),
            pltpu.VMEM((10, 4, PK, BLK), F32),
            pltpu.VMEM((10, 4, PK, BLK), F32),
            pltpu.VMEM((10, PK, BLK), F32),
            pltpu.VMEM((2, 10, PK, BLK), F32),
            pltpu.VMEM((10, PK, BLK), F32),
            pltpu.VMEM((2, NZ, PK, BLK), F32),
            dma((10,)), dma((10,)), dma((10,)), dma((10,)), dma((2, 10)), dma((2, 10)),
            dma((10,)), dma((2, NZ)),
        ],
        compiler_params=pltpu.CompilerParams(collective_id=0, has_side_effects=True,
                                             vmem_limit_bytes=24 * 2**20),
        name="reduce",
    )(names, xs)


def unpack(p):
    row, lane = iota((64, BLK), 0), iota((64, BLK), 1)
    body, corner = p[:64], p[64:]
    top = jnp.where(row < lane, body, 0.0)
    low = jnp.where((row > lane), body, 0.0)
    bottom = pltpu.roll(low, 64, 1)
    off = jnp.concatenate([top, bottom], axis=0)
    diag_top = jnp.where(row == lane, body, 0.0)
    diag_bottom = jnp.where(lane - 64 == row, jnp.concatenate([corner] * 8, axis=0), 0.0)
    return off + off.T + jnp.concatenate([diag_top, diag_bottom], axis=0)


def mm(a, b):
    return jnp.dot(a.astype(BF16), b.astype(BF16), preferred_element_type=F32)


def mm32(a, b):
    return jnp.dot(a, b, preferred_element_type=F32, precision=HI)


def inverse_kernel(table, pa, pg, gvec, prev, out, kept, m_ref, x_ref, ksem):
    keep = pltpu.make_async_copy(prev, kept, ksem)
    keep.start()
    s, x, z, c = place()
    r = z * 8 + c * 4 + x
    na, ng = table[80], table[81]
    is_a = r < na
    used = jnp.logical_or(is_a, r >= 64 - ng)
    row, lane = iota((BLK, BLK), 0), iota((BLK, BLK), 1)
    eye = jnp.where(row == lane, 1.0, 0.0).astype(F32)

    @pl.when(jnp.logical_not(used))
    def _():
        out[...] = jnp.zeros_like(out)

    @pl.when(used)
    def _():
        g_row = gvec[0:1]
        g_col = jnp.sum(g_row * eye, axis=1, keepdims=True)
        m = unpack(jnp.where(is_a, pa[...], pg[...])) * (1.0 / TOKENS)
        m = m * g_row * g_col + damping * eye
        d = jnp.where(row == lane, lax.rsqrt(m), 0.0)
        d_row = jnp.sum(d, axis=0, keepdims=True)
        d_col = jnp.sum(d, axis=1, keepdims=True)
        m = m * d_row * d_col
        m_ref[...] = m
        top = jnp.max(jnp.sum(jnp.abs(m), axis=0, keepdims=True), axis=1, keepdims=True)
        alpha = 1.8 / top
        p = eye - alpha * m
        y = eye + p
        for _ in range(6):
            p = mm(p, p)
            y = y + mm(y, p)
        y = alpha * y
        y = 0.5 * (y + y.T)
        e = eye - mm32(m, y)
        y = y + mm(y, e)
        e = eye - mm32(m, y)
        worst = jnp.max(jnp.abs(e))
        y = y + mm(y, e)
        y = 0.5 * (y + y.T)
        out[...] = (y * d_row * d_col).astype(BF16)

        @pl.when(jnp.logical_not(worst < 1e-3))
        def _():
            x_ref[...] = m_ref[...]

            def sweep(k, _):
                a = x_ref[...]
                r_k = x_ref[pl.ds(k, 1), :]
                c_k = jnp.sum(jnp.where(lane == k, a, 0.0), axis=1, keepdims=True)
                piv = jnp.sum(jnp.where(iota((1, BLK), 1) == k, r_k, 0.0), axis=1, keepdims=True)
                inv = 1.0 / piv
                new = a - c_k * (r_k * inv)
                new = jnp.where(row == k, r_k * inv, new)
                new = jnp.where(lane == k, c_k * inv, new)
                new = jnp.where(jnp.logical_and(row == k, lane == k), -inv, new)
                x_ref[...] = new
                return 0

            lax.fori_loop(0, BLK, sweep, 0)
            y = x_ref[...]
            y = -0.5 * (y + y.T)
            out[...] = (y * d_row * d_col).astype(BF16)

    keep.wait()


def inverse(table, pa, pg, gvec, prev):
    vmem = pl.BlockSpec(memory_space=pltpu.VMEM)
    return pl.pallas_call(
        inverse_kernel,
        out_shape=(pltpu.VMEM((BLK, BLK), BF16), pltpu.VMEM((2 * NBLK, BLK, BLK), BF16)),
        in_specs=[pl.BlockSpec(memory_space=pltpu.SMEM), vmem, vmem, vmem, pl.BlockSpec(memory_space=pl.ANY)],
        out_specs=(vmem, vmem),
        scratch_shapes=[pltpu.VMEM((BLK, BLK), F32), pltpu.VMEM((BLK, BLK), F32), pltpu.SemaphoreType.DMA],
        compiler_params=pltpu.CompilerParams(vmem_limit_bytes=8 * 2**20),
        name="inverse",
    )(table, pa, pg, gvec, pltpu.with_memory_space_constraint(prev, pltpu.HBM))


def gather_kernel(mine, out, zr, nr, fr, cr, sent):
    s, x, z, c = place()
    mate = dev(s, x, z, 1 - c)
    right, left, across = lax.rem(x + 1, NX), lax.rem(x + 3, NX), lax.rem(x + 2, NX)
    sides = [dev(s, right, z, c), dev(s, left, z, c)]
    greet([mate] + sides + [dev(s, x, lax.rem(z + d, NZ), c) for d in range(1, NZ)])
    out[c, x, z] = mine[...]
    order = (0, 1, 7, 2, 6, 3, 5, 4)

    def along(d):
        to = dev(s, x, lax.rem(z + d, NZ), c)
        return remote(out.at[c, x, z], out.at[c, x, z], sent, zr.at[d], to)

    def block(xf, i):
        return out.at[c, xf, lax.rem(z - order[i] + NZ, NZ)]

    def beside(i, w):
        return remote(block(x, i), block(x, i), sent, nr.at[w, i], sides[w])

    def came(i, w):
        at = block((left, right)[w], i)
        return at, remote(at, at, sent, nr.at[w, i], sides[w])

    def on(i):
        w = i % 2
        at = block((left, right)[w], i)
        return remote(at, at, sent, fr.at[i], sides[w])

    def pair(xf, i):
        at = block(xf, i)
        return remote(at, at, sent, cr, mate)

    for d in order[1:]:
        along(d).start()

    def first(i):
        d = order[i]
        if d:
            at = block(x, i)
            remote(at, at, sent, zr.at[d], mate).wait_recv()
        beside(i, 0).start()
        beside(i, 1).start()
        pair(x, i).start()

    def second(i):
        w = i % 2
        came(i, w)[1].wait_recv()
        on(i).start()
        pair((left, right)[w], i).start()
        came(i, 1 - w)[1].wait_recv()
        pair((right, left)[w], i).start()

    def third(i):
        at = block(across, i)
        remote(at, at, sent, fr.at[i], mate).wait_recv()
        pair(across, i).start()

    for i in range(12):
        if i < 8:
            first(i)
        if 2 <= i < 10:
            second(i - 2)
        if i >= 4:
            third(i - 4)

    half = out.at[1 - c]
    remote(half, half, sent, cr, mate).wait_recv()
    remote(half, half, sent, cr, mate).wait_send()
    rest = out.at[c, 0:3]
    remote(rest, rest, sent, cr, mate).wait_send()
    rest = out.at[c, 0, 0:7]
    remote(rest, rest, sent, cr, mate).wait_send()


def gather(mine):
    dma = pltpu.SemaphoreType.DMA
    shape = (NC, NX, NZ, BLK, BLK)
    vmem = pl.BlockSpec(memory_space=pltpu.VMEM)
    return pl.pallas_call(
        gather_kernel,
        out_shape=pltpu.VMEM(shape, BF16),
        in_specs=[vmem],
        out_specs=vmem,
        scratch_shapes=[dma((8,)), dma((2, 8)), dma((8,)), dma, dma],
        compiler_params=pltpu.CompilerParams(collective_id=1, has_side_effects=True,
                                             vmem_limit_bytes=8 * 2**20),
        name="gather",
    )(mine)


def scatter_kernel(table, fresh, kept, out, buf, sems):
    step = 16

    def write(n):
        rows = pl.ds(n * step, step)
        return pltpu.make_async_copy(buf.at[rows], out.at[rows], sems.at[n])

    for n in range(2 * NBLK // step):
        for i in range(n * step, (n + 1) * step):
            at = table[i]

            @pl.when(at >= 0)
            def _():
                buf[i] = fresh[at]

            @pl.when(at < 0)
            def _():
                buf[i] = kept[i]

        write(n).start()
    for n in range(2 * NBLK // step):
        write(n).wait()


def scatter(table, fresh, kept):
    vmem = pl.BlockSpec(memory_space=pltpu.VMEM)
    shape = (2 * NBLK, BLK, BLK)
    return pl.pallas_call(
        scatter_kernel,
        out_shape=pltpu.HBM(shape, BF16),
        in_specs=[pl.BlockSpec(memory_space=pltpu.SMEM), vmem, vmem],
        out_specs=pl.BlockSpec(memory_space=pl.ANY),
        scratch_shapes=[pltpu.VMEM(shape, BF16), pltpu.SemaphoreType.DMA((5,))],
        compiler_params=pltpu.CompilerParams(vmem_limit_bytes=8 * 2**20),
        name="scatter",
    )(table, fresh, kept)


def body(layer_out, input_grad, embedded, loss_grad, norm_gain, prev_inverse, plan):
    names, table, gvec, xs = load(plan.transpose(2, 0, 1), layer_out[0], input_grad[0], embedded, loss_grad,
                                  norm_gain)
    pa, pg = reduce(names, xs)
    mine, kept = inverse(table, pa, pg, gvec, prev_inverse.reshape(2 * NBLK, BLK, BLK))
    every = gather(mine).reshape(64, BLK, BLK)
    return scatter(table, every, kept).reshape(prev_inverse.shape)


def solution(mesh):
    in_specs = (
        P("section", "dp", None),
        P("section", "dp", None),
        P("dp", None),
        P("dp", None),
        P("section", None),
        P("section", None, None, None, None),
        P(),
    )
    out_specs = P("section", None, None, None, None)
    return jax.shard_map(body, mesh=mesh, in_specs=in_specs, out_specs=out_specs, check_vma=False)
```

```python
import functools

import jax
import jax.numpy as jnp
from jax import lax
from jax.experimental import pallas as pl
from jax.experimental.pallas import tpu as pltpu
from jax.sharding import PartitionSpec as P

BLK = 128
NBLK = 40
ENTRIES = 128
NX, NZ, NC = 4, 8, 2
LEV = 5
PK = 72
ROWS = 256
RELAYED = 7
TOKENS = 16384
damping = 0.1
MESH = pl.DeviceIdType.MESH
F32 = jnp.float32
BF16 = jnp.bfloat16
HI = lax.Precision.HIGHEST


def iota(shape, dim):
    return lax.broadcasted_iota(jnp.int32, shape, dim)


def pack(g):
    top, bottom = g[:64], g[64:]
    row, lane = iota((64, BLK), 0), iota((64, BLK), 1)
    turned = pltpu.roll(bottom, 64, 1)
    body = jnp.where((lane < 64) & (row > lane), turned, top)
    diag = jnp.where(lane - 64 == row, bottom, 0.0)
    corner = diag[0:8]
    for v in range(1, 8):
        corner = corner + diag[8 * v:8 * v + 8]
    return body, corner


def chunk_of(r, g):
    z = r >> 3
    q = jnp.where(z == 3, 4, z + 2) if g else jnp.where(z == 4, 5, z)
    return (((r >> 2) & 1) * 10 + q) * 4 + (r & 3)


def place():
    dp = lax.axis_index("dp")
    return lax.axis_index("section"), lax.div(dp, 16), lax.rem(lax.div(dp, 2), 8), lax.rem(dp, 2)


def dev(s, x, z, c):
    return (s, (x * NZ + z) * NC + c)


def greet(targets):
    barrier = pltpu.get_barrier_semaphore()
    for t in targets:
        pl.semaphore_signal(barrier, inc=1, device_id=t, device_id_type=MESH)
    pl.semaphore_wait(barrier, len(targets))


def remote(src, dst, ssem, rsem, to):
    return pltpu.make_async_remote_copy(src_ref=src, dst_ref=dst, send_sem=ssem, recv_sem=rsem,
                                        device_id=to, device_id_type=MESH)


def z_of(q):
    g = jnp.logical_or(q == 4, q >= 6)
    return jnp.where(q <= 3, q, jnp.where(q <= 4, 3, jnp.where(q <= 6, 4, q - 2))), jnp.where(g, 1, 0)


def look_up(code, s, my_slot):
    square = (BLK, BLK)
    down, over = iota(square, 0), iota(square, 1)
    row = jnp.broadcast_to(code, square)
    col = row.T
    kind, k = col >> 6, col & 63
    earlier = jnp.logical_and(kind == (row >> 6), down < over)
    rank_row = jnp.sum(jnp.where(earlier, 1, 0), axis=0, keepdims=True)
    rank = jnp.broadcast_to(rank_row, square).T
    here_a, here_g = kind == ((s + 1) & 3) * 2, kind == ((s + 3) & 3) * 2 + 1
    at = jnp.where(here_a, chunk_of(rank, 0), jnp.where(here_g, chunk_of(63 - rank, 1), -1))
    names = jnp.sum(jnp.where(at == over, k, 0), axis=0, keepdims=True)
    mine_a, mine_g = kind == s * 2, kind == s * 2 + 1
    slot = jnp.where(mine_a, rank, 63 - rank)
    spot = ((slot >> 2) & 1) * 32 + (slot & 3) * 8 + (slot >> 3) + 1
    key = jnp.where(mine_a, k, jnp.where(mine_g, NBLK + k, -1))
    table = jnp.sum(jnp.where(key == over, spot, 0), axis=0, keepdims=True) - 1
    na = jnp.sum(jnp.where(mine_a, 1, 0), axis=0, keepdims=True)
    ng = jnp.sum(jnp.where(mine_g, 1, 0), axis=0, keepdims=True)
    lane = iota((1, BLK), 1)
    table = jnp.where(lane == 80, na, jnp.where(lane == 81, ng, table))
    my_k = jnp.sum(jnp.where(jnp.logical_and(mine_a, rank == my_slot), k + 1, 0), axis=0, keepdims=True) - 1
    return names, table, my_k


def reduce_kernel(plan_at, gain_at, layer_out, input_grad, embedded, loss_grad, out_a, out_g, table, gvec,
                  plan, gain, found_v, names, psem, gsem, nsem, tsem,
                  xa, xs, away, own, rc, d2, near, s2, rz, sems, xsem, cs, cr, ds, dr, ns, nr, zs, zr):
    s, x, z, c = place()
    quarter = ROWS // 4
    listed = pltpu.make_async_copy(plan_at, plan, psem)
    listed.start()
    gains = pltpu.make_async_copy(gain_at, gain, gsem)
    gains.start()

    def fetch(i, src):
        rows = pl.ds(i * quarter, quarter)
        return pltpu.make_async_copy(src.at[rows], xa.at[rows], sems.at[i])

    def stripes(src):
        for b in range(NBLK):
            pltpu.make_async_copy(src.at[:, b * BLK:(b + 1) * BLK], xs.at[1, b], xsem).start()

    @pl.when(s == 3)
    def _():
        for i in range(4):
            fetch(i, embedded).start()

    @pl.when(s != 3)
    def _():
        for i in range(4):
            fetch(i, layer_out).start()

    @pl.when(s == 0)
    def _():
        stripes(loss_grad)

    @pl.when(s != 0)
    def _():
        stripes(input_grad)

    mate = dev(s, x, z, 1 - c)
    right, left = lax.rem(x + 1, NX), lax.rem(x + 3, NX)
    across = lax.rem(x + 2, NX)
    ahead, behind = lax.rem(s + 1, 4), lax.rem(s + 3, 4)
    has_a, has_g = z < LEV, z >= NZ - LEV
    barrier = pltpu.get_barrier_semaphore()

    def hail(t):
        pl.semaphore_signal(barrier, inc=1, device_id=t, device_id_type=MESH)

    for t in (mate, dev(s, right, z, c), dev(s, left, z, c), dev(s, across, z, c)):
        hail(t)

    @pl.when(has_a)
    def _():
        for zf in range(NZ):
            hail(dev(behind, x, zf, c))

    @pl.when(has_g)
    def _():
        for zf in range(NZ):
            hail(dev(ahead, x, zf, c))

    zfirst = lax.rem(z + 2, NZ)
    q0 = jnp.where(zfirst <= 3, zfirst, jnp.where(zfirst == 4, 5, zfirst + 2))

    def way(i):
        w = lax.rem(i, 2)
        return jnp.where(w == 0, right, left), jnp.where(w == 0, left, right), w

    def core(i):
        return remote(away.at[i], rc.at[i], cs.at[i], cr.at[i], mate)

    def far(i):
        to = jnp.where(i < RELAYED, way(i)[0], across)
        return remote(rc.at[i, across], d2.at[i], ds.at[i], dr.at[i], dev(s, to, z, c))

    def beside(i, xt, w):
        return remote(rc.at[i, xt], near.at[w, i], ns.at[w, i], nr.at[w, i], dev(s, xt, z, c))

    def up(i):
        zt, g = z_of(lax.rem(q0 + i, 10))
        to = dev(jnp.where(g == 0, ahead, behind), x, zt, c)
        return remote(s2.at[i], rz.at[g, z], zs.at[i], zr.at[g, z], to)

    dims = (((0,), (0,)), ((), ()))

    def grams(i, cc, into):
        q = lax.rem(q0 + i, 10)
        g = z_of(q)[1]
        found = []
        for xt in range(NX):
            k = names[0, (cc * 10 + q) * 4 + xt]
            col = xs[g, k]
            found.append(lax.dot_general(col, col, dims, preferred_element_type=F32))
        for xt in range(NX):
            body, corner = pack(found[xt])
            into[i, xt, 0:64] = body
            into[i, xt, 64:72] = corner

    def first(i):
        core(i).wait_recv()
        one, other, w = way(i)
        rc[i, across] = rc[i, across] + own[i, across]
        far(i).start()
        rc[i, other] = rc[i, other] + own[i, other]
        beside(i, other, 1 - w).start()
        rc[i, one] = rc[i, one] + own[i, one]

        @pl.when(i >= RELAYED)
        def _():
            beside(i, one, w).start()

        rc[i, x] = rc[i, x] + own[i, x]

    def second(i):
        far(i).wait_recv()
        one, _, w = way(i)
        to = jnp.where(i < RELAYED, one, x)
        rc[i, to] = rc[i, to] + d2[i]

        @pl.when(i < RELAYED)
        def _():
            beside(i, one, w).start()

    def third(i):
        beside(i, right, 0).wait_recv()
        beside(i, left, 1).wait_recv()
        s2[i] = rc[i, x] + (near[0, i] + near[1, i])
        up(i).start()

    listed.wait()
    parts = [plan[0, t:t + 1] * 128 + plan[1, t:t + 1] * 64 + plan[2, t:t + 1] for t in range(4)]
    named, tabled, my_k = look_up(jnp.concatenate(parts, axis=1), s, z * 8 + c * 4 + x)
    found_v[0] = named
    found_v[1] = tabled
    to_names = pltpu.make_async_copy(found_v.at[0], names, nsem)
    to_names.start()
    to_table = pltpu.make_async_copy(found_v.at[1], table, tsem)
    to_table.start()
    gains.wait()
    scaled = jnp.where(my_k < 0, 1.0, 0.0)
    for b in range(NBLK):
        scaled = jnp.where(my_k == b, gain[:, b * BLK:(b + 1) * BLK].astype(F32), scaled)
    gvec[...] = jnp.broadcast_to(scaled, (8, BLK))

    def norm(start, q, _):
        rows = pl.ds(pl.multiple_of(start + q * 32, 32), 32)
        acc = [jnp.zeros((32, BLK), F32) for _ in range(2)]
        for b in range(NBLK):
            v = xa[rows, b * BLK:(b + 1) * BLK].astype(F32)
            acc[b % 2] = acc[b % 2] + v * v
        mean = jnp.sum(acc[0] + acc[1], axis=1, keepdims=True) / (NBLK * BLK)
        scale = jnp.broadcast_to(lax.rsqrt(mean + 1e-05), (32, BLK))
        for b in range(NBLK):
            v = xa[rows, b * BLK:(b + 1) * BLK].astype(F32)
            xs[0, b, rows, :] = (v * scale).astype(BF16)
        return 0

    for i in range(4):
        fetch(i, layer_out).wait()
        lax.fori_loop(0, quarter // 32, functools.partial(norm, i * quarter), 0)
    pltpu.make_async_copy(xs.at[0], xs.at[1], xsem).wait()

    to_names.wait()
    to_table.wait()
    grams(0, 1 - c, away)
    grams(1, 1 - c, away)
    pl.semaphore_wait(barrier, 14)
    core(0).start()
    core(1).start()

    def step(i, _):
        @pl.when(i < 8)
        def _():
            grams(i + 2, 1 - c, away)
            core(i + 2).start()

        @pl.when(i < 10)
        def _():
            grams(i, c, own)
            first(i)

        @pl.when(jnp.logical_and(i >= 2, i < 12))
        def _():
            second(i - 2)

        @pl.when(i >= 4)
        def _():
            third(i - 4)

        return 0

    lax.fori_loop(0, 14, step, 0)

    def total(g, out):
        for zf in range(NZ):
            remote(s2.at[0], rz.at[g, zf], zs.at[0], zr.at[g, zf], mate).wait_recv()
        out[...] = ((rz[g, 0] + rz[g, 1]) + (rz[g, 2] + rz[g, 3])) + ((rz[g, 4] + rz[g, 5]) + (rz[g, 6] + rz[g, 7]))

    @pl.when(has_a)
    def _():
        total(0, out_a)

    @pl.when(jnp.logical_not(has_a))
    def _():
        out_a[...] = jnp.zeros_like(out_a)

    @pl.when(has_g)
    def _():
        total(1, out_g)

    @pl.when(jnp.logical_not(has_g))
    def _():
        out_g[...] = jnp.zeros_like(out_g)

    def sent(i, _):
        core(i).wait_send()
        far(i).wait_send()
        beside(i, right, 0).wait_send()
        beside(i, left, 1).wait_send()
        up(i).wait_send()
        return 0

    lax.fori_loop(0, 10, sent, 0)


def reduce(*given):
    any_ = pl.BlockSpec(memory_space=pl.ANY)
    vmem = pl.BlockSpec(memory_space=pltpu.VMEM)
    blk = pltpu.VMEM((PK, BLK), F32)
    dma = pltpu.SemaphoreType.DMA
    return pl.pallas_call(
        reduce_kernel,
        out_shape=(blk, blk, pltpu.SMEM((1, BLK), jnp.int32), pltpu.VMEM((8, BLK), F32)),
        in_specs=[any_] * 6,
        out_specs=(vmem, vmem, pl.BlockSpec(memory_space=pltpu.SMEM), vmem),
        scratch_shapes=[
            pltpu.VMEM((3, 4, 32), jnp.int32),
            pltpu.VMEM((1, NBLK * BLK), BF16),
            pltpu.VMEM((2, 1, BLK), jnp.int32),
            pltpu.SMEM((1, BLK), jnp.int32),
            dma, dma, dma, dma,
            pltpu.VMEM((ROWS, NBLK * BLK), BF16),
            pltpu.VMEM((2, NBLK, ROWS, BLK), BF16),
            pltpu.VMEM((10, 4, PK, BLK), F32),
            pltpu.VMEM((10, 4, PK, BLK), F32),
            pltpu.VMEM((10, 4, PK, BLK), F32),
            pltpu.VMEM((10, PK, BLK), F32),
            pltpu.VMEM((2, 10, PK, BLK), F32),
            pltpu.VMEM((10, PK, BLK), F32),
            pltpu.VMEM((2, NZ, PK, BLK), F32),
            dma((4,)), dma,
            dma((10,)), dma((10,)), dma((10,)), dma((10,)), dma((2, 10)), dma((2, 10)),
            dma((10,)), dma((2, NZ)),
        ],
        compiler_params=pltpu.CompilerParams(collective_id=0, has_side_effects=True,
                                             vmem_limit_bytes=32 * 2**20),
        name="reduce",
    )(*(pltpu.with_memory_space_constraint(a, pltpu.HBM) for a in given))


def unpack(p):
    row, lane = iota((64, BLK), 0), iota((64, BLK), 1)
    body, corner = p[:64], p[64:]
    top = jnp.where(row < lane, body, 0.0)
    low = jnp.where((row > lane), body, 0.0)
    bottom = pltpu.roll(low, 64, 1)
    off = jnp.concatenate([top, bottom], axis=0)
    diag_top = jnp.where(row == lane, body, 0.0)
    diag_bottom = jnp.where(lane - 64 == row, jnp.concatenate([corner] * 8, axis=0), 0.0)
    return off + off.T + jnp.concatenate([diag_top, diag_bottom], axis=0)


def mm(a, b):
    return jnp.dot(a.astype(BF16), b.astype(BF16), preferred_element_type=F32)


def mm32(a, b):
    return jnp.dot(a, b, preferred_element_type=F32, precision=HI)


def inverse_kernel(table, pa, pg, gvec, prev, out, kept, m_ref, x_ref, ksem):
    keep = pltpu.make_async_copy(prev, kept, ksem)
    keep.start()
    s, x, z, c = place()
    r = z * 8 + c * 4 + x
    na, ng = table[0, 80], table[0, 81]
    is_a = r < na
    used = jnp.logical_or(is_a, r >= 64 - ng)
    row, lane = iota((BLK, BLK), 0), iota((BLK, BLK), 1)
    eye = jnp.where(row == lane, 1.0, 0.0).astype(F32)

    @pl.when(jnp.logical_not(used))
    def _():
        out[...] = jnp.zeros_like(out)

    @pl.when(used)
    def _():
        g_row = gvec[0:1]
        g_col = jnp.sum(g_row * eye, axis=1, keepdims=True)
        m = unpack(jnp.where(is_a, pa[...], pg[...])) * (1.0 / TOKENS)
        m = m * g_row * g_col + damping * eye
        d = jnp.where(row == lane, lax.rsqrt(m), 0.0)
        d_row = jnp.sum(d, axis=0, keepdims=True)
        d_col = jnp.sum(d, axis=1, keepdims=True)
        m = m * d_row * d_col
        m_ref[...] = m
        top = jnp.max(jnp.sum(jnp.abs(m), axis=0, keepdims=True), axis=1, keepdims=True)
        alpha = 1.8 / top
        p = eye - alpha * m
        y = eye + p
        for _ in range(6):
            p = mm(p, p)
            y = y + mm(y, p)
        y = alpha * y
        y = 0.5 * (y + y.T)
        e = eye - mm32(m, y)
        y = y + mm(y, e)
        e = eye - mm32(m, y)
        worst = jnp.max(jnp.abs(e))
        y = y + mm(y, e)
        y = 0.5 * (y + y.T)
        out[...] = (y * d_row * d_col).astype(BF16)

        @pl.when(jnp.logical_not(worst < 1e-3))
        def _():
            x_ref[...] = m_ref[...]

            def sweep(k, _):
                a = x_ref[...]
                r_k = x_ref[pl.ds(k, 1), :]
                c_k = jnp.sum(jnp.where(lane == k, a, 0.0), axis=1, keepdims=True)
                piv = jnp.sum(jnp.where(iota((1, BLK), 1) == k, r_k, 0.0), axis=1, keepdims=True)
                inv = 1.0 / piv
                new = a - c_k * (r_k * inv)
                new = jnp.where(row == k, r_k * inv, new)
                new = jnp.where(lane == k, c_k * inv, new)
                new = jnp.where(jnp.logical_and(row == k, lane == k), -inv, new)
                x_ref[...] = new
                return 0

            lax.fori_loop(0, BLK, sweep, 0)
            y = x_ref[...]
            y = -0.5 * (y + y.T)
            out[...] = (y * d_row * d_col).astype(BF16)

    keep.wait()


def inverse(table, pa, pg, gvec, prev):
    vmem = pl.BlockSpec(memory_space=pltpu.VMEM)
    return pl.pallas_call(
        inverse_kernel,
        out_shape=(pltpu.VMEM((BLK, BLK), BF16), pltpu.VMEM((2 * NBLK, BLK, BLK), BF16)),
        in_specs=[pl.BlockSpec(memory_space=pltpu.SMEM), vmem, vmem, vmem, pl.BlockSpec(memory_space=pl.ANY)],
        out_specs=(vmem, vmem),
        scratch_shapes=[pltpu.VMEM((BLK, BLK), F32), pltpu.VMEM((BLK, BLK), F32), pltpu.SemaphoreType.DMA],
        compiler_params=pltpu.CompilerParams(vmem_limit_bytes=8 * 2**20),
        name="inverse",
    )(table, pa, pg, gvec, pltpu.with_memory_space_constraint(prev, pltpu.HBM))


def gather_kernel(mine, out, zr, nr, fr, cr, sent):
    s, x, z, c = place()
    mate = dev(s, x, z, 1 - c)
    right, left, across = lax.rem(x + 1, NX), lax.rem(x + 3, NX), lax.rem(x + 2, NX)
    sides = [dev(s, right, z, c), dev(s, left, z, c)]
    greet([mate, dev(s, across, z, c)] + sides + [dev(s, x, lax.rem(z + d, NZ), c) for d in range(1, NZ)])
    out[c, x, z] = mine[...]
    order = (0, 1, 7, 2, 6, 3, 5, 4)

    def along(d):
        to = dev(s, x, lax.rem(z + d, NZ), c)
        return remote(out.at[c, x, z], out.at[c, x, z], sent, zr.at[d], to)

    def block(xf, i):
        return out.at[c, xf, lax.rem(z - order[i] + NZ, NZ)]

    def beside(i, w):
        return remote(block(x, i), block(x, i), sent, nr.at[w, i], sides[w])

    def came(i, w):
        at = block((left, right)[w], i)
        return at, remote(at, at, sent, nr.at[w, i], sides[w])

    def on(i):
        w = i % 2
        at = block(x if i >= 5 else (left, right)[w], i)
        return remote(at, at, sent, fr.at[i], dev(s, across, z, c) if i >= 5 else sides[w])

    def pair(xf, i):
        at = block(xf, i)
        return remote(at, at, sent, cr, mate)

    for d in order[1:]:
        along(d).start()

    def first(i):
        d = order[i]
        if d:
            at = block(x, i)
            remote(at, at, sent, zr.at[d], mate).wait_recv()
        if i >= 5:
            on(i).start()
        beside(i, 0).start()
        beside(i, 1).start()
        pair(x, i).start()

    def second(i):
        w = i % 2
        came(i, w)[1].wait_recv()
        if i < 5:
            on(i).start()
        pair((left, right)[w], i).start()
        came(i, 1 - w)[1].wait_recv()
        pair((right, left)[w], i).start()

    def third(i):
        at = block(across, i)
        remote(at, at, sent, fr.at[i], mate).wait_recv()
        pair(across, i).start()

    for step, i in ((first, 0), (first, 1), (first, 2), (second, 0), (first, 3), (first, 4), (second, 1), (second, 2),
                    (first, 5), (first, 6), (third, 0), (second, 3), (second, 4), (first, 7), (third, 1), (third, 2),
                    (second, 5), (second, 6), (third, 3), (third, 4), (third, 5), (third, 6), (second, 7), (third, 7)):
        step(i)

    half = out.at[1 - c]
    remote(half, half, sent, cr, mate).wait_recv()
    remote(half, half, sent, cr, mate).wait_send()
    rest = out.at[c, 0:3]
    remote(rest, rest, sent, cr, mate).wait_send()
    rest = out.at[c, 0, 0:7]
    remote(rest, rest, sent, cr, mate).wait_send()


def gather(mine):
    dma = pltpu.SemaphoreType.DMA
    shape = (NC, NX, NZ, BLK, BLK)
    vmem = pl.BlockSpec(memory_space=pltpu.VMEM)
    return pl.pallas_call(
        gather_kernel,
        out_shape=pltpu.VMEM(shape, BF16),
        in_specs=[vmem],
        out_specs=vmem,
        scratch_shapes=[dma((8,)), dma((2, 8)), dma((8,)), dma, dma],
        compiler_params=pltpu.CompilerParams(collective_id=1, has_side_effects=True,
                                             vmem_limit_bytes=8 * 2**20),
        name="gather",
    )(mine)


def scatter_kernel(table, fresh, kept, out, buf, sems):
    step = 16

    def write(n):
        rows = pl.ds(n * step, step)
        return pltpu.make_async_copy(buf.at[rows], out.at[rows], sems.at[n])

    for n in range(2 * NBLK // step):
        for i in range(n * step, (n + 1) * step):
            at = table[0, i]

            @pl.when(at >= 0)
            def _():
                buf[i] = fresh[at]

            @pl.when(at < 0)
            def _():
                buf[i] = kept[i]

        write(n).start()
    for n in range(2 * NBLK // step):
        write(n).wait()


def scatter(table, fresh, kept):
    vmem = pl.BlockSpec(memory_space=pltpu.VMEM)
    shape = (2 * NBLK, BLK, BLK)
    return pl.pallas_call(
        scatter_kernel,
        out_shape=pltpu.HBM(shape, BF16),
        in_specs=[pl.BlockSpec(memory_space=pltpu.SMEM), vmem, vmem],
        out_specs=pl.BlockSpec(memory_space=pl.ANY),
        scratch_shapes=[pltpu.VMEM(shape, BF16), pltpu.SemaphoreType.DMA((5,))],
        compiler_params=pltpu.CompilerParams(vmem_limit_bytes=8 * 2**20),
        name="scatter",
    )(table, fresh, kept)


def body(layer_out, input_grad, embedded, loss_grad, norm_gain, prev_inverse, plan):
    pa, pg, table, gvec = reduce(plan.transpose(2, 0, 1), norm_gain, layer_out[0], input_grad[0], embedded, loss_grad)
    mine, kept = inverse(table, pa, pg, gvec, prev_inverse.reshape(2 * NBLK, BLK, BLK))
    every = gather(mine).reshape(64, BLK, BLK)
    return scatter(table, every, kept).reshape(prev_inverse.shape)


def solution(mesh):
    in_specs = (
        P("section", "dp", None),
        P("section", "dp", None),
        P("dp", None),
        P("dp", None),
        P("section", None),
        P("section", None, None, None, None),
        P(),
    )
    out_specs = P("section", None, None, None, None)
    return jax.shard_map(body, mesh=mesh, in_specs=in_specs, out_specs=out_specs, check_vma=False)
```

```python
import functools

import jax
import jax.numpy as jnp
from jax import lax
from jax.experimental import pallas as pl
from jax.experimental.pallas import tpu as pltpu
from jax.sharding import PartitionSpec as P

BLK = 128
NBLK = 40
ENTRIES = 128
NX, NZ, NC = 4, 8, 2
LEV = 5
PK = 72
ROWS = 256
RELAYED = 7
TOKENS = 16384
damping = 0.1
MESH = pl.DeviceIdType.MESH
F32 = jnp.float32
BF16 = jnp.bfloat16
HI = lax.Precision.HIGHEST


def iota(shape, dim):
    return lax.broadcasted_iota(jnp.int32, shape, dim)


def pack(g):
    top, bottom = g[:64], g[64:]
    row, lane = iota((64, BLK), 0), iota((64, BLK), 1)
    turned = pltpu.roll(bottom, 64, 1)
    body = jnp.where((lane < 64) & (row > lane), turned, top)
    diag = jnp.where(lane - 64 == row, bottom, 0.0)
    corner = diag[0:8]
    for v in range(1, 8):
        corner = corner + diag[8 * v:8 * v + 8]
    return body, corner


def chunk_of(r, g):
    z = r >> 3
    q = jnp.where(z == 3, 4, z + 2) if g else jnp.where(z == 4, 5, z)
    return (((r >> 2) & 1) * 10 + q) * 4 + (r & 3)


def place():
    dp = lax.axis_index("dp")
    return lax.axis_index("section"), lax.div(dp, 16), lax.rem(lax.div(dp, 2), 8), lax.rem(dp, 2)


def dev(s, x, z, c):
    return (s, (x * NZ + z) * NC + c)


def greet(targets):
    barrier = pltpu.get_barrier_semaphore()
    for t in targets:
        pl.semaphore_signal(barrier, inc=1, device_id=t, device_id_type=MESH)
    pl.semaphore_wait(barrier, len(targets))


def remote(src, dst, ssem, rsem, to):
    return pltpu.make_async_remote_copy(src_ref=src, dst_ref=dst, send_sem=ssem, recv_sem=rsem,
                                        device_id=to, device_id_type=MESH)


def z_of(q):
    g = jnp.logical_or(q == 4, q >= 6)
    return jnp.where(q <= 3, q, jnp.where(q <= 4, 3, jnp.where(q <= 6, 4, q - 2))), jnp.where(g, 1, 0)


def look_up(code, s, my_slot):
    square = (BLK, BLK)
    down, over = iota(square, 0), iota(square, 1)
    row = jnp.broadcast_to(code, square)
    col = row.T
    kind, k = col >> 6, col & 63
    earlier = jnp.logical_and(kind == (row >> 6), down < over)
    rank_row = jnp.sum(jnp.where(earlier, 1, 0), axis=0, keepdims=True)
    rank = jnp.broadcast_to(rank_row, square).T
    here_a, here_g = kind == ((s + 1) & 3) * 2, kind == ((s + 3) & 3) * 2 + 1
    at = jnp.where(here_a, chunk_of(rank, 0), jnp.where(here_g, chunk_of(63 - rank, 1), -1))
    names = jnp.sum(jnp.where(at == over, k, 0), axis=0, keepdims=True)
    mine_a, mine_g = kind == s * 2, kind == s * 2 + 1
    slot = jnp.where(mine_a, rank, 63 - rank)
    spot = ((slot >> 2) & 1) * 32 + (slot & 3) * 8 + (slot >> 3) + 1
    key = jnp.where(mine_a, k, jnp.where(mine_g, NBLK + k, -1))
    table = jnp.sum(jnp.where(key == over, spot, 0), axis=0, keepdims=True) - 1
    na = jnp.sum(jnp.where(mine_a, 1, 0), axis=0, keepdims=True)
    ng = jnp.sum(jnp.where(mine_g, 1, 0), axis=0, keepdims=True)
    lane = iota((1, BLK), 1)
    table = jnp.where(lane == 80, na, jnp.where(lane == 81, ng, table))
    my_k = jnp.sum(jnp.where(jnp.logical_and(mine_a, rank == my_slot), k + 1, 0), axis=0, keepdims=True) - 1
    return names, table, my_k


def reduce_kernel(plan_at, gain_at, layer_out, input_grad, embedded, loss_grad, out_a, out_g, table, gvec,
                  plan, gain, found_v, names, psem, gsem, nsem, tsem,
                  xa, xs, away, own, rc, d2, near, s2, rz, sems, xsem, cr, dr, nr, zr, gone):
    s, x, z, c = place()
    quarter = ROWS // 4
    listed = pltpu.make_async_copy(plan_at, plan, psem)
    listed.start()
    gains = pltpu.make_async_copy(gain_at, gain, gsem)
    gains.start()

    def fetch(i, src):
        rows = pl.ds(i * quarter, quarter)
        return pltpu.make_async_copy(src.at[rows], xa.at[rows], sems.at[i])

    def stripes(src):
        for b in range(NBLK):
            pltpu.make_async_copy(src.at[:, b * BLK:(b + 1) * BLK], xs.at[1, b], xsem).start()

    @pl.when(s == 3)
    def _():
        for i in range(4):
            fetch(i, embedded).start()

    @pl.when(s != 3)
    def _():
        for i in range(4):
            fetch(i, layer_out).start()

    @pl.when(s == 0)
    def _():
        stripes(loss_grad)

    @pl.when(s != 0)
    def _():
        stripes(input_grad)

    mate = dev(s, x, z, 1 - c)
    right, left = lax.rem(x + 1, NX), lax.rem(x + 3, NX)
    across = lax.rem(x + 2, NX)
    ahead, behind = lax.rem(s + 1, 4), lax.rem(s + 3, 4)
    has_a, has_g = z < LEV, z >= NZ - LEV
    barrier = pltpu.get_barrier_semaphore()

    def hail(t):
        pl.semaphore_signal(barrier, inc=1, device_id=t, device_id_type=MESH)

    for t in (mate, dev(s, right, z, c), dev(s, left, z, c), dev(s, across, z, c)):
        hail(t)

    @pl.when(has_a)
    def _():
        for zf in range(NZ):
            hail(dev(behind, x, zf, c))

    @pl.when(has_g)
    def _():
        for zf in range(NZ):
            hail(dev(ahead, x, zf, c))

    zfirst = lax.rem(z + 2, NZ)
    q0 = jnp.where(zfirst <= 3, zfirst, jnp.where(zfirst == 4, 5, zfirst + 2))

    def way(i):
        w = lax.rem(i, 2)
        return jnp.where(w == 0, right, left), jnp.where(w == 0, left, right), w

    def core(i):
        return remote(away.at[i], rc.at[i], gone, cr.at[i], mate)

    def far(i):
        to = jnp.where(i < RELAYED, way(i)[0], across)
        return remote(rc.at[i, across], d2.at[i], gone, dr.at[i], dev(s, to, z, c))

    def beside(i, xt, w):
        return remote(rc.at[i, xt], near.at[w, i], gone, nr.at[w, i], dev(s, xt, z, c))

    def up(i):
        zt, g = z_of(lax.rem(q0 + i, 10))
        to = dev(jnp.where(g == 0, ahead, behind), x, zt, c)
        return remote(s2.at[i], rz.at[g, z], gone, zr.at[g], to)

    dims = (((0,), (0,)), ((), ()))

    def grams(i, cc, into):
        q = lax.rem(q0 + i, 10)
        g = z_of(q)[1]
        found = []
        for xt in range(NX):
            k = names[0, (cc * 10 + q) * 4 + xt]
            col = xs[g, k]
            found.append(lax.dot_general(col, col, dims, preferred_element_type=F32))
        for xt in range(NX):
            body, corner = pack(found[xt])
            into[i, xt, 0:64] = body
            into[i, xt, 64:72] = corner

    def first(i):
        core(i).wait_recv()
        one, other, w = way(i)
        rc[i, across] = rc[i, across] + own[i, across]
        far(i).start()
        rc[i, other] = rc[i, other] + own[i, other]
        beside(i, other, 1 - w).start()
        rc[i, one] = rc[i, one] + own[i, one]

        @pl.when(i >= RELAYED)
        def _():
            beside(i, one, w).start()

        rc[i, x] = rc[i, x] + own[i, x]

    def second(i):
        far(i).wait_recv()
        one, _, w = way(i)
        to = jnp.where(i < RELAYED, one, x)
        rc[i, to] = rc[i, to] + d2[i]

        @pl.when(i < RELAYED)
        def _():
            beside(i, one, w).start()

    def third(i):
        beside(i, right, 0).wait_recv()
        beside(i, left, 1).wait_recv()
        s2[i] = rc[i, x] + (near[0, i] + near[1, i])
        up(i).start()

    listed.wait()
    parts = [plan[0, t:t + 1] * 128 + plan[1, t:t + 1] * 64 + plan[2, t:t + 1] for t in range(4)]
    named, tabled, my_k = look_up(jnp.concatenate(parts, axis=1), s, z * 8 + c * 4 + x)
    found_v[0] = named
    found_v[1] = tabled
    to_names = pltpu.make_async_copy(found_v.at[0], names, nsem)
    to_names.start()
    to_table = pltpu.make_async_copy(found_v.at[1], table, tsem)
    to_table.start()
    gains.wait()
    scaled = jnp.where(my_k < 0, 1.0, 0.0)
    for b in range(NBLK):
        scaled = jnp.where(my_k == b, gain[:, b * BLK:(b + 1) * BLK].astype(F32), scaled)
    gvec[...] = jnp.broadcast_to(scaled, (8, BLK))

    def norm(start, q, _):
        rows = pl.ds(pl.multiple_of(start + q * 32, 32), 32)
        acc = [jnp.zeros((32, BLK), F32) for _ in range(2)]
        for b in range(NBLK):
            v = xa[rows, b * BLK:(b + 1) * BLK].astype(F32)
            acc[b % 2] = acc[b % 2] + v * v
        mean = jnp.sum(acc[0] + acc[1], axis=1, keepdims=True) / (NBLK * BLK)
        scale = jnp.broadcast_to(lax.rsqrt(mean + 1e-05), (32, BLK))
        for b in range(NBLK):
            v = xa[rows, b * BLK:(b + 1) * BLK].astype(F32)
            xs[0, b, rows, :] = (v * scale).astype(BF16)
        return 0

    for i in range(4):
        fetch(i, layer_out).wait()
        lax.fori_loop(0, quarter // 32, functools.partial(norm, i * quarter), 0)
    pltpu.make_async_copy(xs.at[0], xs.at[1], xsem).wait()

    to_names.wait()
    to_table.wait()
    grams(0, 1 - c, away)
    grams(1, 1 - c, away)
    pl.semaphore_wait(barrier, 14)
    core(0).start()
    core(1).start()

    def step(i, _):
        @pl.when(i < 8)
        def _():
            grams(i + 2, 1 - c, away)
            core(i + 2).start()

        @pl.when(i < 10)
        def _():
            grams(i, c, own)
            first(i)

        @pl.when(jnp.logical_and(i >= 2, i < 12))
        def _():
            second(i - 2)

        @pl.when(i >= 4)
        def _():
            third(i - 4)

        return 0

    lax.fori_loop(0, 14, step, 0)

    def total(g, out):
        remote(rz.at[g], rz.at[g], gone, zr.at[g], mate).wait_recv()
        out[...] = ((rz[g, 0] + rz[g, 1]) + (rz[g, 2] + rz[g, 3])) + ((rz[g, 4] + rz[g, 5]) + (rz[g, 6] + rz[g, 7]))

    @pl.when(has_a)
    def _():
        total(0, out_a)

    @pl.when(jnp.logical_not(has_a))
    def _():
        out_a[...] = jnp.zeros_like(out_a)

    @pl.when(has_g)
    def _():
        total(1, out_g)

    @pl.when(jnp.logical_not(has_g))
    def _():
        out_g[...] = jnp.zeros_like(out_g)

    remote(own, own, gone, cr.at[0], mate).wait_send()
    remote(own, own, gone, cr.at[0], mate).wait_send()


def reduce(*given):
    any_ = pl.BlockSpec(memory_space=pl.ANY)
    vmem = pl.BlockSpec(memory_space=pltpu.VMEM)
    blk = pltpu.VMEM((PK, BLK), F32)
    dma = pltpu.SemaphoreType.DMA
    return pl.pallas_call(
        reduce_kernel,
        out_shape=(blk, blk, pltpu.SMEM((1, BLK), jnp.int32), pltpu.VMEM((8, BLK), F32)),
        in_specs=[any_] * 6,
        out_specs=(vmem, vmem, pl.BlockSpec(memory_space=pltpu.SMEM), vmem),
        scratch_shapes=[
            pltpu.VMEM((3, 4, 32), jnp.int32),
            pltpu.VMEM((1, NBLK * BLK), BF16),
            pltpu.VMEM((2, 1, BLK), jnp.int32),
            pltpu.SMEM((1, BLK), jnp.int32),
            dma, dma, dma, dma,
            pltpu.VMEM((ROWS, NBLK * BLK), BF16),
            pltpu.VMEM((2, NBLK, ROWS, BLK), BF16),
            pltpu.VMEM((10, 4, PK, BLK), F32),
            pltpu.VMEM((10, 4, PK, BLK), F32),
            pltpu.VMEM((10, 4, PK, BLK), F32),
            pltpu.VMEM((10, PK, BLK), F32),
            pltpu.VMEM((2, 10, PK, BLK), F32),
            pltpu.VMEM((10, PK, BLK), F32),
            pltpu.VMEM((2, NZ, PK, BLK), F32),
            dma((4,)), dma,
            dma((10,)), dma((10,)), dma((2, 10)), dma((2,)), dma,
        ],
        compiler_params=pltpu.CompilerParams(collective_id=0, has_side_effects=True,
                                             vmem_limit_bytes=32 * 2**20),
        name="reduce",
    )(*(pltpu.with_memory_space_constraint(a, pltpu.HBM) for a in given))


def unpack(p):
    row, lane = iota((64, BLK), 0), iota((64, BLK), 1)
    body, corner = p[:64], p[64:]
    top = jnp.where(row < lane, body, 0.0)
    low = jnp.where((row > lane), body, 0.0)
    bottom = pltpu.roll(low, 64, 1)
    off = jnp.concatenate([top, bottom], axis=0)
    diag_top = jnp.where(row == lane, body, 0.0)
    diag_bottom = jnp.where(lane - 64 == row, jnp.concatenate([corner] * 8, axis=0), 0.0)
    return off + off.T + jnp.concatenate([diag_top, diag_bottom], axis=0)


def mm(a, b):
    return jnp.dot(a.astype(BF16), b.astype(BF16), preferred_element_type=F32)


def mm32(a, b):
    return jnp.dot(a, b, preferred_element_type=F32, precision=HI)


def inverse_kernel(table, pa, pg, gvec, prev, out, kept, m_ref, x_ref, ksem):
    keep = pltpu.make_async_copy(prev, kept, ksem)
    keep.start()
    s, x, z, c = place()
    r = z * 8 + c * 4 + x
    na, ng = table[0, 80], table[0, 81]
    is_a = r < na
    used = jnp.logical_or(is_a, r >= 64 - ng)
    row, lane = iota((BLK, BLK), 0), iota((BLK, BLK), 1)
    eye = jnp.where(row == lane, 1.0, 0.0).astype(F32)

    @pl.when(jnp.logical_not(used))
    def _():
        out[...] = jnp.zeros_like(out)

    @pl.when(used)
    def _():
        g_row = gvec[0:1]
        g_col = jnp.sum(g_row * eye, axis=1, keepdims=True)
        m = unpack(jnp.where(is_a, pa[...], pg[...])) * (1.0 / TOKENS)
        m = m * g_row * g_col + damping * eye
        d = jnp.where(row == lane, lax.rsqrt(m), 0.0)
        d_row = jnp.sum(d, axis=0, keepdims=True)
        d_col = jnp.sum(d, axis=1, keepdims=True)
        m = m * d_row * d_col
        m_ref[...] = m
        top = jnp.max(jnp.sum(jnp.abs(m), axis=0, keepdims=True), axis=1, keepdims=True)
        alpha = 1.8 / top
        p = eye - alpha * m
        y = eye + p
        for _ in range(6):
            p = mm(p, p)
            y = y + mm(y, p)
        y = alpha * y
        y = 0.5 * (y + y.T)
        e = eye - mm32(m, y)
        y = y + mm(y, e)
        e = eye - mm32(m, y)
        worst = jnp.max(jnp.abs(e))
        y = y + mm(y, e)
        y = 0.5 * (y + y.T)
        out[...] = (y * d_row * d_col).astype(BF16)

        @pl.when(jnp.logical_not(worst < 1e-3))
        def _():
            x_ref[...] = m_ref[...]

            def sweep(k, _):
                a = x_ref[...]
                r_k = x_ref[pl.ds(k, 1), :]
                c_k = jnp.sum(jnp.where(lane == k, a, 0.0), axis=1, keepdims=True)
                piv = jnp.sum(jnp.where(iota((1, BLK), 1) == k, r_k, 0.0), axis=1, keepdims=True)
                inv = 1.0 / piv
                new = a - c_k * (r_k * inv)
                new = jnp.where(row == k, r_k * inv, new)
                new = jnp.where(lane == k, c_k * inv, new)
                new = jnp.where(jnp.logical_and(row == k, lane == k), -inv, new)
                x_ref[...] = new
                return 0

            lax.fori_loop(0, BLK, sweep, 0)
            y = x_ref[...]
            y = -0.5 * (y + y.T)
            out[...] = (y * d_row * d_col).astype(BF16)

    keep.wait()


def inverse(table, pa, pg, gvec, prev):
    vmem = pl.BlockSpec(memory_space=pltpu.VMEM)
    return pl.pallas_call(
        inverse_kernel,
        out_shape=(pltpu.VMEM((BLK, BLK), BF16), pltpu.VMEM((2 * NBLK, BLK, BLK), BF16)),
        in_specs=[pl.BlockSpec(memory_space=pltpu.SMEM), vmem, vmem, vmem, pl.BlockSpec(memory_space=pl.ANY)],
        out_specs=(vmem, vmem),
        scratch_shapes=[pltpu.VMEM((BLK, BLK), F32), pltpu.VMEM((BLK, BLK), F32), pltpu.SemaphoreType.DMA],
        compiler_params=pltpu.CompilerParams(vmem_limit_bytes=8 * 2**20),
        name="inverse",
    )(table, pa, pg, gvec, pltpu.with_memory_space_constraint(prev, pltpu.HBM))


def gather_kernel(mine, out, zr, nr, fr, cr, sent):
    s, x, z, c = place()
    mate = dev(s, x, z, 1 - c)
    right, left, across = lax.rem(x + 1, NX), lax.rem(x + 3, NX), lax.rem(x + 2, NX)
    sides = [dev(s, right, z, c), dev(s, left, z, c)]
    greet([mate, dev(s, across, z, c)] + sides + [dev(s, x, lax.rem(z + d, NZ), c) for d in range(1, NZ)])
    out[c, x, z] = mine[...]
    order = (0, 1, 7, 2, 6, 3, 5, 4)

    def along(d):
        to = dev(s, x, lax.rem(z + d, NZ), c)
        return remote(out.at[c, x, z], out.at[c, x, z], sent, zr.at[d], to)

    def block(xf, i):
        return out.at[c, xf, lax.rem(z - order[i] + NZ, NZ)]

    def beside(i, w):
        return remote(block(x, i), block(x, i), sent, nr.at[w, i], sides[w])

    def came(i, w):
        at = block((left, right)[w], i)
        return at, remote(at, at, sent, nr.at[w, i], sides[w])

    def on(i):
        w = i % 2
        at = block(x if i >= 5 else (left, right)[w], i)
        return remote(at, at, sent, fr.at[i], dev(s, across, z, c) if i >= 5 else sides[w])

    def pair(xf, i):
        at = block(xf, i)
        return remote(at, at, sent, cr, mate)

    for d in order[1:]:
        along(d).start()

    def first(i):
        d = order[i]
        if d:
            at = block(x, i)
            remote(at, at, sent, zr.at[d], mate).wait_recv()
        if i >= 5:
            on(i).start()
        beside(i, 0).start()
        beside(i, 1).start()
        pair(x, i).start()

    def second(i):
        w = i % 2
        came(i, w)[1].wait_recv()
        if i < 5:
            on(i).start()
        pair((left, right)[w], i).start()
        came(i, 1 - w)[1].wait_recv()
        pair((right, left)[w], i).start()

    def third(i):
        at = block(across, i)
        remote(at, at, sent, fr.at[i], mate).wait_recv()
        pair(across, i).start()

    for step, i in ((first, 0), (first, 1), (first, 2), (second, 0), (first, 3), (first, 4), (second, 1), (second, 2),
                    (first, 5), (first, 6), (third, 0), (second, 3), (second, 4), (first, 7), (third, 1), (third, 2),
                    (second, 5), (second, 6), (third, 3), (third, 4), (third, 5), (third, 6), (second, 7), (third, 7)):
        step(i)

    half = out.at[1 - c]
    remote(half, half, sent, cr, mate).wait_recv()
    remote(half, half, sent, cr, mate).wait_send()
    rest = out.at[c, 0:3]
    remote(rest, rest, sent, cr, mate).wait_send()
    rest = out.at[c, 0, 0:7]
    remote(rest, rest, sent, cr, mate).wait_send()


def gather(mine):
    dma = pltpu.SemaphoreType.DMA
    shape = (NC, NX, NZ, BLK, BLK)
    vmem = pl.BlockSpec(memory_space=pltpu.VMEM)
    return pl.pallas_call(
        gather_kernel,
        out_shape=pltpu.VMEM(shape, BF16),
        in_specs=[vmem],
        out_specs=vmem,
        scratch_shapes=[dma((8,)), dma((2, 8)), dma((8,)), dma, dma],
        compiler_params=pltpu.CompilerParams(collective_id=1, has_side_effects=True,
                                             vmem_limit_bytes=8 * 2**20),
        name="gather",
    )(mine)


def scatter_kernel(table, fresh, kept, out, buf, sems):
    step = 16

    def write(n):
        rows = pl.ds(n * step, step)
        return pltpu.make_async_copy(buf.at[rows], out.at[rows], sems.at[n])

    for n in range(2 * NBLK // step):
        for i in range(n * step, (n + 1) * step):
            at = table[0, i]

            buf[i] = jnp.where(at >= 0, fresh[lax.max(at, 0)], kept[i])

        write(n).start()
    for n in range(2 * NBLK // step):
        write(n).wait()


def scatter(table, fresh, kept):
    vmem = pl.BlockSpec(memory_space=pltpu.VMEM)
    shape = (2 * NBLK, BLK, BLK)
    return pl.pallas_call(
        scatter_kernel,
        out_shape=pltpu.HBM(shape, BF16),
        in_specs=[pl.BlockSpec(memory_space=pltpu.SMEM), vmem, vmem],
        out_specs=pl.BlockSpec(memory_space=pl.ANY),
        scratch_shapes=[pltpu.VMEM(shape, BF16), pltpu.SemaphoreType.DMA((5,))],
        compiler_params=pltpu.CompilerParams(vmem_limit_bytes=8 * 2**20),
        name="scatter",
    )(table, fresh, kept)


def body(layer_out, input_grad, embedded, loss_grad, norm_gain, prev_inverse, plan):
    pa, pg, table, gvec = reduce(plan.transpose(2, 0, 1), norm_gain, layer_out[0], input_grad[0], embedded, loss_grad)
    mine, kept = inverse(table, pa, pg, gvec, prev_inverse.reshape(2 * NBLK, BLK, BLK))
    every = gather(mine).reshape(64, BLK, BLK)
    return scatter(table, every, kept).reshape(prev_inverse.shape)


def solution(mesh):
    in_specs = (
        P("section", "dp", None),
        P("section", "dp", None),
        P("dp", None),
        P("dp", None),
        P("section", None),
        P("section", None, None, None, None),
        P(),
    )
    out_specs = P("section", None, None, None, None)
    return jax.shard_map(body, mesh=mesh, in_specs=in_specs, out_specs=out_specs, check_vma=False)
```

```python
import functools

import jax
import jax.numpy as jnp
from jax import lax
from jax.experimental import pallas as pl
from jax.experimental.pallas import tpu as pltpu
from jax.sharding import PartitionSpec as P

BLK = 128
NBLK = 40
ENTRIES = 128
NX, NZ, NC = 4, 8, 2
LEV = 5
PK = 72
ROWS = 256
RELAYED = 7
TOKENS = 16384
damping = 0.1
MESH = pl.DeviceIdType.MESH
F32 = jnp.float32
BF16 = jnp.bfloat16
HI = lax.Precision.HIGHEST


def iota(shape, dim):
    return lax.broadcasted_iota(jnp.int32, shape, dim)


def pack(g):
    top, bottom = g[:64], g[64:]
    row, lane = iota((64, BLK), 0), iota((64, BLK), 1)
    turned = pltpu.roll(bottom, 64, 1)
    body = jnp.where((lane < 64) & (row > lane), turned, top)
    diag = jnp.where(lane - 64 == row, bottom, 0.0)
    corner = diag[0:8]
    for v in range(1, 8):
        corner = corner + diag[8 * v:8 * v + 8]
    return body, corner


def chunk_of(r, g):
    z = r >> 3
    q = jnp.where(z == 3, 4, z + 2) if g else jnp.where(z == 4, 5, z)
    return (((r >> 2) & 1) * 10 + q) * 4 + (r & 3)


def place():
    dp = lax.axis_index("dp")
    return lax.axis_index("section"), lax.div(dp, 16), lax.rem(lax.div(dp, 2), 8), lax.rem(dp, 2)


def dev(s, x, z, c):
    return (s, (x * NZ + z) * NC + c)


def greet(targets):
    barrier = pltpu.get_barrier_semaphore()
    for t in targets:
        pl.semaphore_signal(barrier, inc=1, device_id=t, device_id_type=MESH)
    pl.semaphore_wait(barrier, len(targets))


def remote(src, dst, ssem, rsem, to):
    return pltpu.make_async_remote_copy(src_ref=src, dst_ref=dst, send_sem=ssem, recv_sem=rsem,
                                        device_id=to, device_id_type=MESH)


def z_of(q):
    g = jnp.logical_or(q == 4, q >= 6)
    return jnp.where(q <= 3, q, jnp.where(q <= 4, 3, jnp.where(q <= 6, 4, q - 2))), jnp.where(g, 1, 0)


def look_up(code, s, my_slot):
    square = (BLK, BLK)
    down, over = iota(square, 0), iota(square, 1)
    row = jnp.broadcast_to(code, square)
    col = row.T
    kind, k = col >> 6, col & 63
    earlier = jnp.logical_and(kind == (row >> 6), down < over)
    rank_row = jnp.sum(jnp.where(earlier, 1, 0), axis=0, keepdims=True)
    rank = jnp.broadcast_to(rank_row, square).T
    here_a, here_g = kind == ((s + 1) & 3) * 2, kind == ((s + 3) & 3) * 2 + 1
    at = jnp.where(here_a, chunk_of(rank, 0), jnp.where(here_g, chunk_of(63 - rank, 1), -1))
    names = jnp.sum(jnp.where(at == over, k, 0), axis=0, keepdims=True)
    mine_a, mine_g = kind == s * 2, kind == s * 2 + 1
    slot = jnp.where(mine_a, rank, 63 - rank)
    spot = ((slot >> 2) & 1) * 32 + (slot & 3) * 8 + (slot >> 3) + 1
    key = jnp.where(mine_a, k, jnp.where(mine_g, NBLK + k, -1))
    table = jnp.sum(jnp.where(key == over, spot, 0), axis=0, keepdims=True) - 1
    na = jnp.sum(jnp.where(mine_a, 1, 0), axis=0, keepdims=True)
    ng = jnp.sum(jnp.where(mine_g, 1, 0), axis=0, keepdims=True)
    lane = iota((1, BLK), 1)
    table = jnp.where(lane == 80, na, jnp.where(lane == 81, ng, table))
    my_k = jnp.sum(jnp.where(jnp.logical_and(mine_a, rank == my_slot), k + 1, 0), axis=0, keepdims=True) - 1
    return names, table, my_k


def reduce_kernel(plan_at, gain_at, layer_out, input_grad, embedded, loss_grad, out_a, out_g, table, gvec,
                  plan, gain, found_v, names, psem, gsem, nsem, tsem,
                  xa, xs, away, own, rc, d2, near, s2, rz, sems, xsem, cr, dr, nr, zr, gone):
    s, x, z, c = place()
    quarter = ROWS // 4
    listed = pltpu.make_async_copy(plan_at, plan, psem)
    listed.start()
    gains = pltpu.make_async_copy(gain_at, gain, gsem)
    gains.start()

    def fetch(i, src):
        rows = pl.ds(i * quarter, quarter)
        return pltpu.make_async_copy(src.at[rows], xa.at[rows], sems.at[i])

    def stripes(src):
        for b in range(NBLK):
            pltpu.make_async_copy(src.at[:, b * BLK:(b + 1) * BLK], xs.at[1, b], xsem).start()

    @pl.when(s == 3)
    def _():
        for i in range(4):
            fetch(i, embedded).start()

    @pl.when(s != 3)
    def _():
        for i in range(4):
            fetch(i, layer_out).start()

    mate = dev(s, x, z, 1 - c)
    right, left = lax.rem(x + 1, NX), lax.rem(x + 3, NX)
    across = lax.rem(x + 2, NX)
    ahead, behind = lax.rem(s + 1, 4), lax.rem(s + 3, 4)
    has_a, has_g = z < LEV, z >= NZ - LEV
    barrier = pltpu.get_barrier_semaphore()

    def hail(t):
        pl.semaphore_signal(barrier, inc=1, device_id=t, device_id_type=MESH)

    @pl.when(has_a)
    def _():
        for zf in range(NZ):
            hail(dev(behind, x, zf, c))

    @pl.when(has_g)
    def _():
        for zf in range(NZ):
            hail(dev(ahead, x, zf, c))

    for t in (mate, dev(s, right, z, c), dev(s, left, z, c), dev(s, across, z, c)):
        hail(t)

    @pl.when(s == 0)
    def _():
        stripes(loss_grad)

    @pl.when(s != 0)
    def _():
        stripes(input_grad)

    zfirst = lax.rem(z + 2, NZ)
    q0 = jnp.where(zfirst <= 3, zfirst, jnp.where(zfirst == 4, 5, zfirst + 2))

    def way(i):
        w = lax.rem(i, 2)
        return jnp.where(w == 0, right, left), jnp.where(w == 0, left, right), w

    def core(i):
        return remote(away.at[i], rc.at[i], gone, cr.at[i], mate)

    def far(i):
        to = jnp.where(i < RELAYED, way(i)[0], across)
        return remote(rc.at[i, across], d2.at[i], gone, dr.at[i], dev(s, to, z, c))

    def beside(i, xt, w):
        return remote(rc.at[i, xt], near.at[w, i], gone, nr.at[w, i], dev(s, xt, z, c))

    def up(i):
        zt, g = z_of(lax.rem(q0 + i, 10))
        to = dev(jnp.where(g == 0, ahead, behind), x, zt, c)
        return remote(s2.at[i], rz.at[g, z], gone, zr.at[g], to)

    dims = (((0,), (0,)), ((), ()))

    def grams(i, cc, into):
        q = lax.rem(q0 + i, 10)
        g = z_of(q)[1]
        found = []
        for xt in range(NX):
            k = names[0, (cc * 10 + q) * 4 + xt]
            col = xs[g, k]
            found.append(lax.dot_general(col, col, dims, preferred_element_type=F32))
        for xt in range(NX):
            body, corner = pack(found[xt])
            into[i, xt, 0:64] = body
            into[i, xt, 64:72] = corner

    def first(i):
        core(i).wait_recv()
        one, other, w = way(i)
        rc[i, across] = rc[i, across] + own[i, across]
        far(i).start()
        rc[i, other] = rc[i, other] + own[i, other]
        beside(i, other, 1 - w).start()
        rc[i, one] = rc[i, one] + own[i, one]

        @pl.when(i >= RELAYED)
        def _():
            beside(i, one, w).start()

        rc[i, x] = rc[i, x] + own[i, x]

    def second(i):
        far(i).wait_recv()
        one, _, w = way(i)
        to = jnp.where(i < RELAYED, one, x)
        rc[i, to] = rc[i, to] + d2[i]

        @pl.when(i < RELAYED)
        def _():
            beside(i, one, w).start()

    def third(i):
        beside(i, right, 0).wait_recv()
        beside(i, left, 1).wait_recv()
        s2[i] = rc[i, x] + (near[0, i] + near[1, i])
        up(i).start()

    listed.wait()
    parts = [plan[0, t:t + 1] * 128 + plan[1, t:t + 1] * 64 + plan[2, t:t + 1] for t in range(4)]
    named, tabled, my_k = look_up(jnp.concatenate(parts, axis=1), s, z * 8 + c * 4 + x)
    found_v[0] = named
    found_v[1] = tabled
    to_names = pltpu.make_async_copy(found_v.at[0], names, nsem)
    to_names.start()
    to_table = pltpu.make_async_copy(found_v.at[1], table, tsem)
    to_table.start()
    gains.wait()
    scaled = jnp.where(my_k < 0, 1.0, 0.0)
    for b in range(NBLK):
        scaled = jnp.where(my_k == b, gain[:, b * BLK:(b + 1) * BLK].astype(F32), scaled)
    gvec[...] = jnp.broadcast_to(scaled, (8, BLK))

    def norm(start, q, _):
        rows = pl.ds(pl.multiple_of(start + q * 32, 32), 32)
        acc = [jnp.zeros((32, BLK), F32) for _ in range(2)]
        for b in range(NBLK):
            v = xa[rows, b * BLK:(b + 1) * BLK].astype(F32)
            acc[b % 2] = acc[b % 2] + v * v
        mean = jnp.sum(acc[0] + acc[1], axis=1, keepdims=True) / (NBLK * BLK)
        scale = jnp.broadcast_to(lax.rsqrt(mean + 1e-05), (32, BLK))
        for b in range(NBLK):
            v = xa[rows, b * BLK:(b + 1) * BLK].astype(F32)
            xs[0, b, rows, :] = (v * scale).astype(BF16)
        return 0

    for i in range(4):
        fetch(i, layer_out).wait()
        lax.fori_loop(0, quarter // 32, functools.partial(norm, i * quarter), 0)
    pltpu.make_async_copy(xs.at[0], xs.at[1], xsem).wait()

    to_names.wait()
    to_table.wait()
    grams(0, 1 - c, away)
    grams(1, 1 - c, away)
    pl.semaphore_wait(barrier, 14)
    core(0).start()
    core(1).start()

    def step(i, _):
        @pl.when(i < 8)
        def _():
            grams(i + 2, 1 - c, away)
            core(i + 2).start()

        @pl.when(i < 10)
        def _():
            grams(i, c, own)
            first(i)

        @pl.when(jnp.logical_and(i >= 2, i < 12))
        def _():
            second(i - 2)

        @pl.when(i >= 4)
        def _():
            third(i - 4)

        return 0

    lax.fori_loop(0, 14, step, 0)

    def total(g, out):
        remote(rz.at[g], rz.at[g], gone, zr.at[g], mate).wait_recv()
        out[...] = ((rz[g, 0] + rz[g, 1]) + (rz[g, 2] + rz[g, 3])) + ((rz[g, 4] + rz[g, 5]) + (rz[g, 6] + rz[g, 7]))

    @pl.when(has_a)
    def _():
        total(0, out_a)

    @pl.when(jnp.logical_not(has_a))
    def _():
        out_a[...] = jnp.zeros_like(out_a)

    @pl.when(has_g)
    def _():
        total(1, out_g)

    @pl.when(jnp.logical_not(has_g))
    def _():
        out_g[...] = jnp.zeros_like(out_g)

    remote(own, own, gone, cr.at[0], mate).wait_send()
    remote(own, own, gone, cr.at[0], mate).wait_send()


def reduce(*given):
    any_ = pl.BlockSpec(memory_space=pl.ANY)
    vmem = pl.BlockSpec(memory_space=pltpu.VMEM)
    blk = pltpu.VMEM((PK, BLK), F32)
    dma = pltpu.SemaphoreType.DMA
    return pl.pallas_call(
        reduce_kernel,
        out_shape=(blk, blk, pltpu.SMEM((1, BLK), jnp.int32), pltpu.VMEM((8, BLK), F32)),
        in_specs=[any_] * 6,
        out_specs=(vmem, vmem, pl.BlockSpec(memory_space=pltpu.SMEM), vmem),
        scratch_shapes=[
            pltpu.VMEM((3, 4, 32), jnp.int32),
            pltpu.VMEM((1, NBLK * BLK), BF16),
            pltpu.VMEM((2, 1, BLK), jnp.int32),
            pltpu.SMEM((1, BLK), jnp.int32),
            dma, dma, dma, dma,
            pltpu.VMEM((ROWS, NBLK * BLK), BF16),
            pltpu.VMEM((2, NBLK, ROWS, BLK), BF16),
            pltpu.VMEM((10, 4, PK, BLK), F32),
            pltpu.VMEM((10, 4, PK, BLK), F32),
            pltpu.VMEM((10, 4, PK, BLK), F32),
            pltpu.VMEM((10, PK, BLK), F32),
            pltpu.VMEM((2, 10, PK, BLK), F32),
            pltpu.VMEM((10, PK, BLK), F32),
            pltpu.VMEM((2, NZ, PK, BLK), F32),
            dma((4,)), dma,
            dma((10,)), dma((10,)), dma((2, 10)), dma((2,)), dma,
        ],
        compiler_params=pltpu.CompilerParams(collective_id=0, has_side_effects=True,
                                             vmem_limit_bytes=32 * 2**20),
        name="reduce",
    )(*(pltpu.with_memory_space_constraint(a, pltpu.HBM) for a in given))


def unpack(p):
    row, lane = iota((64, BLK), 0), iota((64, BLK), 1)
    body, corner = p[:64], p[64:]
    top = jnp.where(row < lane, body, 0.0)
    low = jnp.where((row > lane), body, 0.0)
    bottom = pltpu.roll(low, 64, 1)
    off = jnp.concatenate([top, bottom], axis=0)
    diag_top = jnp.where(row == lane, body, 0.0)
    diag_bottom = jnp.where(lane - 64 == row, jnp.concatenate([corner] * 8, axis=0), 0.0)
    return off + off.T + jnp.concatenate([diag_top, diag_bottom], axis=0)


def mm(a, b):
    return jnp.dot(a.astype(BF16), b.astype(BF16), preferred_element_type=F32)


def mm32(a, b):
    return jnp.dot(a, b, preferred_element_type=F32, precision=HI)


def inverse_kernel(table, pa, pg, gvec, prev, out, kept, m_ref, x_ref, ksem):
    keep = pltpu.make_async_copy(prev, kept, ksem)
    keep.start()
    s, x, z, c = place()
    r = z * 8 + c * 4 + x
    na, ng = table[0, 80], table[0, 81]
    is_a = r < na
    used = jnp.logical_or(is_a, r >= 64 - ng)
    row, lane = iota((BLK, BLK), 0), iota((BLK, BLK), 1)
    eye = jnp.where(row == lane, 1.0, 0.0).astype(F32)

    @pl.when(jnp.logical_not(used))
    def _():
        out[...] = jnp.zeros_like(out)

    @pl.when(used)
    def _():
        g_row = gvec[0:1]
        g_col = jnp.sum(g_row * eye, axis=1, keepdims=True)
        m = unpack(jnp.where(is_a, pa[...], pg[...])) * (1.0 / TOKENS)
        m = m * g_row * g_col + damping * eye
        d = jnp.where(row == lane, lax.rsqrt(m), 0.0)
        d_row = jnp.sum(d, axis=0, keepdims=True)
        d_col = jnp.sum(d, axis=1, keepdims=True)
        m = m * d_row * d_col
        m_ref[...] = m
        top = jnp.max(jnp.sum(jnp.abs(m), axis=0, keepdims=True), axis=1, keepdims=True)
        alpha = 1.8 / top
        p = eye - alpha * m
        y = eye + p
        for _ in range(6):
            p = mm(p, p)
            y = y + mm(y, p)
        y = alpha * y
        y = 0.5 * (y + y.T)
        e = eye - mm32(m, y)
        y = y + mm(y, e)
        e = eye - mm32(m, y)
        worst = jnp.max(jnp.abs(e))
        y = y + mm(y, e)
        y = 0.5 * (y + y.T)
        out[...] = (y * d_row * d_col).astype(BF16)

        @pl.when(jnp.logical_not(worst < 1e-3))
        def _():
            x_ref[...] = m_ref[...]

            def sweep(k, _):
                a = x_ref[...]
                r_k = x_ref[pl.ds(k, 1), :]
                c_k = jnp.sum(jnp.where(lane == k, a, 0.0), axis=1, keepdims=True)
                piv = jnp.sum(jnp.where(iota((1, BLK), 1) == k, r_k, 0.0), axis=1, keepdims=True)
                inv = 1.0 / piv
                new = a - c_k * (r_k * inv)
                new = jnp.where(row == k, r_k * inv, new)
                new = jnp.where(lane == k, c_k * inv, new)
                new = jnp.where(jnp.logical_and(row == k, lane == k), -inv, new)
                x_ref[...] = new
                return 0

            lax.fori_loop(0, BLK, sweep, 0)
            y = x_ref[...]
            y = -0.5 * (y + y.T)
            out[...] = (y * d_row * d_col).astype(BF16)

    keep.wait()


def inverse(table, pa, pg, gvec, prev):
    vmem = pl.BlockSpec(memory_space=pltpu.VMEM)
    return pl.pallas_call(
        inverse_kernel,
        out_shape=(pltpu.VMEM((BLK, BLK), BF16), pltpu.VMEM((2 * NBLK, BLK, BLK), BF16)),
        in_specs=[pl.BlockSpec(memory_space=pltpu.SMEM), vmem, vmem, vmem, pl.BlockSpec(memory_space=pl.ANY)],
        out_specs=(vmem, vmem),
        scratch_shapes=[pltpu.VMEM((BLK, BLK), F32), pltpu.VMEM((BLK, BLK), F32), pltpu.SemaphoreType.DMA],
        compiler_params=pltpu.CompilerParams(vmem_limit_bytes=8 * 2**20),
        name="inverse",
    )(table, pa, pg, gvec, pltpu.with_memory_space_constraint(prev, pltpu.HBM))


def gather_kernel(mine, out, zr, nr, fr, cr, sent):
    s, x, z, c = place()
    mate = dev(s, x, z, 1 - c)
    right, left, across = lax.rem(x + 1, NX), lax.rem(x + 3, NX), lax.rem(x + 2, NX)
    sides = [dev(s, right, z, c), dev(s, left, z, c)]
    greet([mate, dev(s, across, z, c)] + sides + [dev(s, x, lax.rem(z + d, NZ), c) for d in range(1, NZ)])
    out[c, x, z] = mine[...]
    order = (0, 1, 7, 2, 6, 3, 5, 4)

    def along(d):
        to = dev(s, x, lax.rem(z + d, NZ), c)
        return remote(out.at[c, x, z], out.at[c, x, z], sent, zr.at[d], to)

    def block(xf, i):
        return out.at[c, xf, lax.rem(z - order[i] + NZ, NZ)]

    def beside(i, w):
        return remote(block(x, i), block(x, i), sent, nr.at[w, i], sides[w])

    def came(i, w):
        at = block((left, right)[w], i)
        return at, remote(at, at, sent, nr.at[w, i], sides[w])

    def on(i):
        w = i % 2
        at = block(x if i >= 5 else (left, right)[w], i)
        return remote(at, at, sent, fr.at[i], dev(s, across, z, c) if i >= 5 else sides[w])

    def pair(xf, i):
        at = block(xf, i)
        return remote(at, at, sent, cr, mate)

    for d in order[1:]:
        along(d).start()

    def first(i):
        d = order[i]
        if d:
            at = block(x, i)
            remote(at, at, sent, zr.at[d], mate).wait_recv()
        if i >= 5:
            on(i).start()
        beside(i, 0).start()
        beside(i, 1).start()
        pair(x, i).start()

    def second(i):
        w = i % 2
        came(i, w)[1].wait_recv()
        if i < 5:
            on(i).start()
        pair((left, right)[w], i).start()
        came(i, 1 - w)[1].wait_recv()
        pair((right, left)[w], i).start()

    def third(i):
        at = block(across, i)
        remote(at, at, sent, fr.at[i], mate).wait_recv()
        pair(across, i).start()

    for step, i in ((first, 0), (first, 1), (first, 2), (second, 0), (first, 3), (first, 4), (second, 1), (second, 2),
                    (first, 5), (first, 6), (third, 0), (second, 3), (second, 4), (first, 7), (third, 1), (third, 2),
                    (second, 5), (second, 6), (third, 3), (third, 4), (third, 5), (third, 6), (second, 7), (third, 7)):
        step(i)

    half = out.at[1 - c]
    remote(half, half, sent, cr, mate).wait_recv()
    remote(half, half, sent, cr, mate).wait_send()
    rest = out.at[c, 0:3]
    remote(rest, rest, sent, cr, mate).wait_send()
    rest = out.at[c, 0, 0:7]
    remote(rest, rest, sent, cr, mate).wait_send()


def gather(mine):
    dma = pltpu.SemaphoreType.DMA
    shape = (NC, NX, NZ, BLK, BLK)
    vmem = pl.BlockSpec(memory_space=pltpu.VMEM)
    return pl.pallas_call(
        gather_kernel,
        out_shape=pltpu.VMEM(shape, BF16),
        in_specs=[vmem],
        out_specs=vmem,
        scratch_shapes=[dma((8,)), dma((2, 8)), dma((8,)), dma, dma],
        compiler_params=pltpu.CompilerParams(collective_id=1, has_side_effects=True,
                                             vmem_limit_bytes=8 * 2**20),
        name="gather",
    )(mine)


def scatter_kernel(table, fresh, kept, out, buf, sems):
    step = 16

    def write(n):
        rows = pl.ds(n * step, step)
        return pltpu.make_async_copy(buf.at[rows], out.at[rows], sems.at[n])

    for n in range(2 * NBLK // step):
        for i in range(n * step, (n + 1) * step):
            at = table[0, i]

            buf[i] = jnp.where(at >= 0, fresh[lax.max(at, 0)], kept[i])

        write(n).start()
    for n in range(2 * NBLK // step):
        write(n).wait()


def scatter(table, fresh, kept):
    vmem = pl.BlockSpec(memory_space=pltpu.VMEM)
    shape = (2 * NBLK, BLK, BLK)
    return pl.pallas_call(
        scatter_kernel,
        out_shape=pltpu.HBM(shape, BF16),
        in_specs=[pl.BlockSpec(memory_space=pltpu.SMEM), vmem, vmem],
        out_specs=pl.BlockSpec(memory_space=pl.ANY),
        scratch_shapes=[pltpu.VMEM(shape, BF16), pltpu.SemaphoreType.DMA((5,))],
        compiler_params=pltpu.CompilerParams(vmem_limit_bytes=8 * 2**20),
        name="scatter",
    )(table, fresh, kept)


def body(layer_out, input_grad, embedded, loss_grad, norm_gain, prev_inverse, plan):
    pa, pg, table, gvec = reduce(plan.transpose(2, 0, 1), norm_gain, layer_out[0], input_grad[0], embedded, loss_grad)
    mine, kept = inverse(table, pa, pg, gvec, prev_inverse.reshape(2 * NBLK, BLK, BLK))
    every = gather(mine).reshape(64, BLK, BLK)
    return scatter(table, every, kept).reshape(prev_inverse.shape)


def solution(mesh):
    in_specs = (
        P("section", "dp", None),
        P("section", "dp", None),
        P("dp", None),
        P("dp", None),
        P("section", None),
        P("section", None, None, None, None),
        P(),
    )
    out_specs = P("section", None, None, None, None)
    return jax.shard_map(body, mesh=mesh, in_specs=in_specs, out_specs=out_specs, check_vma=False)
```
